256 devices in a mesh: dp: 8 (over z), nbr: 16 (over x_hi, y, core), mp: 2 (over x_lo).
Axes of the slice: x: 4 (x_hi: 2, x_lo: 2; x = x_hi * 2 + x_lo), y: 4, z: 8, core: 2. Of those that a mesh axis runs over, the one named last changes fastest.
Arguments:
- dec_rows: bfloat16 [8, 4096, 4096], P('dp', 'nbr'), may hold values from -6 to 6
- owner_shift: int32 [8, 4, 2], P('dp'), may hold values from 0 to 15, as said below
- nbr_rows: bfloat16 [8, 128, 128, 1024], P('dp', 'nbr', 'mp'), may hold values from -6 to 6
- cot_attended: bfloat16 [8, 64, 2, 128, 1024], P('dp', 'nbr', None, 'mp'), may hold values from -6 to 6
- query_w: bfloat16 [1024, 512], P(('nbr', 'mp')), may hold values from -0.1875 to 0.1875
- kv_w: bfloat16 [4096, 1024], P(('nbr', 'mp')), may hold values from -0.09375 to 0.09375
- out_w: bfloat16 [512, 1024], P(('nbr', 'mp')), may hold values from -0.25 to 0.25
- pos_bias: float32 [8, 128, 64], replicated, may hold values from -8 to 330
Outputs:
- attended: bfloat16 [8, 64, 2, 128, 1024], P('dp', 'nbr', None, 'mp')
- grad_rows: bfloat16 [8, 4096, 4096], P('dp', ('nbr', 'mp'))
- grad_neigh: bfloat16 [8, 128, 128, 1024], P('dp', 'nbr', 'mp')
- grad_query_w: float32 [1024, 512], P(('nbr', 'mp'))
- grad_out_w: float32 [512, 1024], P(('nbr', 'mp'))
The draws below stay inside these ranges and needn't reach their ends.
Inputs may be any that keep to these rules, and one draw needn't show every extreme that they name: `owner_shift`: within one batch row the 8 shifts are all different.
All inputs are finite; a program needn't handle non-finite values.
Results may differ from the reference program's by a relative error of at most 0.013.
Values may be sent and summed in bfloat16 or wider, within the bound.
A program may use at most 128 MiB of HBM per device.

```python
import jax
import jax.numpy as jnp
from jax import lax

D = 4096
ENC = 1024
HEADS = 8
HDIM = 64
STRETCH = 64
NLEN = 128
NEIGH = 2
STRETCHES = 4
SLOTS = 8
SEQ = 4096
HTOK = 64
N_DP = 8
N_NBR = 16
N_MP = 2


def draw_owner_shift(key, part):
    key = jax.random.fold_in(key, 11)
    row_keys = jax.random.split(key, N_DP)
    orders = jax.vmap(lambda one_key: jax.random.permutation(one_key, N_NBR))(row_keys).astype(jnp.int32)
    row_ids = jnp.arange(N_DP, dtype=jnp.int32)
    target = jnp.where(row_ids == 0, N_NBR - 1, 0)
    rotate = jnp.where(row_ids < 2, target - orders[:, 0], 0)
    orders = (orders + rotate[:, None]) % N_NBR
    return orders[:, :STRETCHES * NEIGH].reshape(N_DP, STRETCHES, NEIGH).astype(jnp.int32)


def draw_pos_bias(key, part):
    key = jax.random.fold_in(key, 23)
    key_base = jax.random.fold_in(key, 0)
    table_shape = (HEADS, NLEN, STRETCH)
    return jnp.clip(2.0 * jax.random.normal(key_base, table_shape, jnp.float32), -8.0, 8.0)


def with_spikes(values, stream_key, source, target, blocks, factor):
    owner, partner = [(jnp.arange(values.shape[axis_at]) // (values.shape[axis_at] // blocks)).reshape([-1 if axis == axis_at else 1 for axis in range(values.ndim)]) for axis_at in (source, target)]
    chosen = jax.random.permutation(stream_key, blocks)[partner]
    strong = (owner == chosen) | (owner == (partner + blocks // 2) % blocks)
    return jnp.where(strong, factor * values, values)


def block_levels(stream_key, dims, cuts, least, top_value):
    gain = 1.0
    for position, blocks in cuts:
        draws = jax.random.uniform(jax.random.fold_in(jax.random.fold_in(stream_key, 6), position), (blocks,), jnp.float32, least / len(cuts), top_value / len(cuts))
        gain = gain * jnp.repeat(jnp.exp(draws), dims[position] // blocks).reshape((-1,) + (1,) * (len(dims) - 1 - position))
    return gain


def centred(stream_key, extent, width, limit, shards=(), held_as=jnp.bfloat16):
    values = width * jax.random.normal(stream_key, extent, jnp.float32)
    if shards:
        values = values * block_levels(stream_key, extent, shards, -0.22, 0.18)
    return jnp.clip(values, -limit, limit).astype(held_as)


def heavy_noise(rng, dims, scale, most, cuts, heavy, kind=jnp.bfloat16):
    values = scale * jax.random.normal(rng, dims, jnp.float32)
    if cuts:
        values = values * block_levels(rng, dims, cuts, -0.22, 0.18)
    return jnp.clip(with_spikes(values, jax.random.fold_in(rng, 3), *heavy), -most, most).astype(kind)


def setup_inputs(seed: int = 0) -> dict:
    streams_of = jax.random.split(jax.random.key(seed), 9)
    dec_rows = centred(streams_of[0], (N_DP, SEQ, D), 1.0, 6.0, ((0, 8), (1, 16)))
    owner_shift = draw_owner_shift(jax.random.fold_in(streams_of[8], 71), 0)
    nbr_rows = heavy_noise(streams_of[2], (N_DP, N_NBR * SLOTS, NLEN, ENC), 1.0, 6.0, ((0, 8), (1, 16), (2, 2)), (1, 3, 16, 2.0))
    cot_attended = centred(streams_of[3], (N_DP, SEQ // STRETCH, NEIGH, NLEN, ENC), 1.0, 6.0, ((0, 8), (1, 16), (3, 2)))
    query_w = centred(streams_of[4], (ENC, HEADS * HDIM), ENC ** -0.5, 0.1875, ((0, 32),))
    kv_w = centred(streams_of[5], (D, 2 * HEADS * HDIM), D ** -0.5, 0.09375, ((0, 32),))
    out_w = centred(streams_of[6], (HEADS * HDIM, ENC), (HEADS * HDIM) ** -0.5, 0.25, ((0, 32),))
    pos_bias = draw_pos_bias(jax.random.fold_in(streams_of[8], 71), 0)
    return {"dec_rows": dec_rows, "owner_shift": owner_shift, "nbr_rows": nbr_rows, "cot_attended": cot_attended, "query_w": query_w, "kv_w": kv_w, "out_w": out_w, "pos_bias": pos_bias}


def round_trip(array):
    return lax.optimization_barrier(array.astype(jnp.bfloat16)).astype(jnp.float32)


def reference(dec_rows, owner_shift, nbr_rows, cot_attended, query_w, kv_w, out_w, pos_bias):
    stretch_total = SEQ // STRETCH
    attn_width = HEADS * HDIM
    owner_ids = jnp.arange(N_NBR, dtype=jnp.int32)
    slot_ids = jnp.arange(SLOTS, dtype=jnp.int32)
    stretch_of = slot_ids // NEIGH
    which_one = slot_ids % NEIGH
    grad_query_w = jnp.zeros((ENC, attn_width), jnp.float32)
    grad_out_w = jnp.zeros((attn_width, ENC), jnp.float32)
    attended_list = []
    rows_list = []
    neigh_list = []
    for batch_row in range(N_DP):
        shifts = owner_shift[batch_row].reshape(SLOTS).astype(jnp.int32)
        source = (owner_ids[:, None] - shifts[None, :]) % N_NBR
        stretch_id = (source * STRETCHES + stretch_of[None, :]).astype(jnp.int32)
        neigh_id = jnp.broadcast_to(which_one[None, :], stretch_id.shape).astype(jnp.int32)
        keys_vals = jnp.dot(dec_rows[batch_row], kv_w, preferred_element_type=jnp.float32).astype(jnp.bfloat16)
        slot_kv = keys_vals.reshape(stretch_total, STRETCH, 2 * attn_width)[stretch_id].astype(jnp.float32)
        key_heads = slot_kv[..., :attn_width].reshape(N_NBR, SLOTS, STRETCH, HEADS, HDIM)
        value_heads = slot_kv[..., attn_width:].reshape(N_NBR, SLOTS, STRETCH, HEADS, HDIM)
        neighbours = nbr_rows[batch_row].reshape(N_NBR * SLOTS * NLEN, ENC)
        queries = jnp.dot(neighbours, query_w, preferred_element_type=jnp.float32)
        query_heads = round_trip(queries).reshape(N_NBR, SLOTS, NLEN, HEADS, HDIM)
        scores = jnp.einsum("osihd,osjhd->oshij", query_heads, key_heads) * 0.125 + pos_bias[None, None]
        row_max = jnp.max(scores, axis=-1, keepdims=True)
        scaled = jnp.exp(scores - row_max)
        weights = scaled / jnp.sum(scaled, axis=-1, keepdims=True)
        probabilities = round_trip(weights)
        mixture = jnp.einsum("oshij,osjhd->osihd", probabilities, value_heads)
        mixture_rows = lax.optimization_barrier(mixture.astype(jnp.bfloat16)).reshape(-1, attn_width)
        result = jnp.dot(mixture_rows, out_w, preferred_element_type=jnp.float32).astype(jnp.bfloat16)
        result = result.reshape(N_NBR, SLOTS, NLEN, ENC)
        attended = jnp.zeros((stretch_total, NEIGH, NLEN, ENC), jnp.bfloat16).at[stretch_id, neigh_id].set(result)
        cot_rows = cot_attended[batch_row][stretch_id, neigh_id].reshape(-1, ENC)
        grad_mixture = jnp.dot(cot_rows, out_w.T, preferred_element_type=jnp.float32)
        grad_heads = round_trip(grad_mixture).reshape(N_NBR, SLOTS, NLEN, HEADS, HDIM)
        grad_out_w = grad_out_w + jnp.dot(mixture_rows.T, cot_rows, preferred_element_type=jnp.float32)
        grad_probs = jnp.einsum("osihd,osjhd->oshij", grad_heads, value_heads)
        grad_scores = round_trip(weights * (grad_probs - jnp.sum(grad_probs * weights, axis=-1, keepdims=True)))
        grad_queries = jnp.einsum("oshij,osjhd->osihd", grad_scores, key_heads) * 0.125
        grad_queries = lax.optimization_barrier(grad_queries.astype(jnp.bfloat16)).reshape(-1, attn_width)
        neigh_grad = jnp.dot(grad_queries, query_w.T, preferred_element_type=jnp.float32).astype(jnp.bfloat16)
        grad_query_w = grad_query_w + jnp.dot(neighbours.T, grad_queries, preferred_element_type=jnp.float32)
        split_scores = grad_scores.reshape(N_NBR, SLOTS, HEADS, N_MP, HTOK, STRETCH)
        split_probs = probabilities.reshape(N_NBR, SLOTS, HEADS, N_MP, HTOK, STRETCH)
        split_queries = query_heads.reshape(N_NBR, SLOTS, N_MP, HTOK, HEADS, HDIM)
        split_grads = grad_heads.reshape(N_NBR, SLOTS, N_MP, HTOK, HEADS, HDIM)
        grad_keys = jnp.einsum("oshpij,ospihd->ospjhd", split_scores, split_queries) * 0.125
        grad_values = jnp.einsum("oshpij,ospihd->ospjhd", split_probs, split_grads)
        grad_kv = jnp.concatenate([grad_keys.reshape(N_NBR, SLOTS, N_MP, STRETCH, attn_width),
                                   grad_values.reshape(N_NBR, SLOTS, N_MP, STRETCH, attn_width)], axis=-1)
        grad_kv = grad_kv.astype(jnp.bfloat16)
        grad_kv_rows = jnp.zeros((stretch_total, NEIGH, N_MP, STRETCH, 2 * attn_width), jnp.bfloat16)
        grad_kv_rows = grad_kv_rows.at[stretch_id, neigh_id].set(grad_kv)
        row_grads = jnp.einsum("gkpjf,df->gjd", grad_kv_rows.astype(jnp.float32), kv_w.astype(jnp.float32))
        attended_list.append(attended)
        rows_list.append(row_grads.astype(jnp.bfloat16).reshape(SEQ, D))
        neigh_list.append(neigh_grad.reshape(N_NBR * SLOTS, NLEN, ENC))
    return (jnp.stack(attended_list), jnp.stack(rows_list), jnp.stack(neigh_list), grad_query_w, grad_out_w)
```

```python
import jax
import jax.numpy as jnp
from jax import lax
from jax.experimental import pallas as pl
from jax.experimental.pallas import tpu as pltpu
from jax.sharding import PartitionSpec as P

BF = jnp.bfloat16
F32 = jnp.float32
MESH = pl.DeviceIdType.MESH


def dot_nn(a, b):
    return lax.dot_general(a, b, (((1,), (0,)), ((), ())), preferred_element_type=F32)


def dot_nt(a, b):
    return lax.dot_general(a, b, (((1,), (1,)), ((), ())), preferred_element_type=F32)


def dot_tn(a, b):
    return lax.dot_general(a, b, (((0,), (0,)), ((), ())), preferred_element_type=F32)


def kernel(
    shift, dec_h, nbr_h, cot_h, wq_h, wkv_h, wo_h, bias_h,
    att_o, rows_o, neigh_o, gqw_o, gow_o,
    qw, kvw, ow, dec, nbr, nbr_t, cot, bias_raw, bias_t,
    queries, qs, qr, kv, gmix, mix, gq_loc, gs, gr, gq_all,
    gkv, gkv_s, gkv_r, att, rows, neigh,
    wred, ored, wr1, or1, wa1, oa1, wr2, or2, wa2, oa2, wr3, or3, zs, zr, za, zg, gqw_v, gow_v,
    lsem, ag_s, ag_r, qx_s, qx_r, gx_s, gx_r, mp_s, mp_r,
    r1_s, r1_r, r2_s, r2_r, r3_s, r3_r, r4_s, r4_r, r5_s, r5_r, osem,
):
    z = lax.axis_index("dp")
    n = lax.axis_index("nbr")
    m = lax.axis_index("mp")
    xh = n // 8
    y = (n // 2) % 4
    c = n % 2
    x = xh * 2 + m

    def at_y(j):
        return {"nbr": xh * 8 + ((y + j) % 4) * 2 + c}

    def at_x(j):
        far = (x + j) % 4
        return {"nbr": (far // 2) * 8 + y * 2 + c, "mp": far % 2}

    def at_z(j):
        return {"dp": (z + j) % 8}

    def at_n(j):
        return {"nbr": (n + j) % 16}

    at_core = {"nbr": xh * 8 + y * 2 + (1 - c)}
    at_mp = {"mp": 1 - m}

    def remote(src, dst, ssem, rsem, device):
        return pltpu.make_async_remote_copy(
            src_ref=src, dst_ref=dst, send_sem=ssem, recv_sem=rsem, device_id=device, device_id_type=MESH
        )

    def each(lo, hi, body):
        lax.fori_loop(lo, hi, lambda j, carry: (body(j), carry)[1], 0)

    local_in = [
        pltpu.make_async_copy(wq_h, qw.at[xh, y, c, m], lsem.at[0]),
        pltpu.make_async_copy(wo_h, ow.at[xh, y, c, m], lsem.at[1]),
        pltpu.make_async_copy(wkv_h, kvw.at[xh, y, c, m], lsem.at[2]),
        pltpu.make_async_copy(nbr_h, nbr, lsem.at[3]),
        pltpu.make_async_copy(cot_h, cot, lsem.at[4]),
        pltpu.make_async_copy(dec_h, dec, lsem.at[5]),
        pltpu.make_async_copy(bias_h, bias_raw, lsem.at[6]),
    ]
    for one in local_in:
        one.start()

    barrier = pltpu.get_barrier_semaphore()
    each(1, 16, lambda j: pl.semaphore_signal(barrier, inc=1, device_id=at_n(j), device_id_type=MESH))
    each(1, 8, lambda j: pl.semaphore_signal(barrier, inc=1, device_id=at_z(j), device_id_type=MESH))
    pl.semaphore_signal(barrier, inc=1, device_id=at_x(1), device_id_type=MESH)
    pl.semaphore_signal(barrier, inc=1, device_id=at_x(3), device_id_type=MESH)
    pl.semaphore_wait(barrier, 24)

    every = slice(None)
    halves = [
        (qw, [(pl.ds(0, 16), every), (pl.ds(16, 16), every)]),
        (ow, [(every, pl.ds(0, 512)), (every, pl.ds(512, 512))]),
        (kvw, [(pl.ds(0, 64), every), (pl.ds(64, 64), every)]),
    ]

    def first(t, h, j, arriving):
        buf, parts = halves[t]
        sy, sx, sm = y, xh, m
        if arriving:
            if h == 0:
                sy = (y + 4 - j) % 4
            else:
                far = (x + 4 - j) % 4
                sx, sm = far // 2, far % 2
        ref = buf.at[(sx, sy, c, sm) + parts[h]]
        return remote(ref, ref, ag_s.at[t, 0, h, j], ag_r.at[t, 0, h, j], at_y(j) if h == 0 else at_x(j))

    def second(t, h, j, arriving):
        buf, parts = halves[t]
        if h == 0:
            far = (x + 4 - j) % 4 if arriving else x
            ref = buf.at[(far // 2, every, c, far % 2) + parts[h]]
        else:
            sy = (y + 4 - j) % 4 if arriving else y
            ref = buf.at[(every, sy, c, every) + parts[h]]
        return remote(ref, ref, ag_s.at[t, 1, h, j], ag_r.at[t, 1, h, j], at_x(j) if h == 0 else at_y(j))

    def third(t, arriving):
        buf = halves[t][0]
        ref = buf.at[:, :, (1 - c) if arriving else c]
        return remote(ref, ref, ag_s.at[t, 2, 0, 0], ag_r.at[t, 2, 0, 0], at_core)

    for t in range(3):
        local_in[t].wait()
        for h in range(2):
            each(1, 4, lambda j, t=t, h=h: first(t, h, j, False).start())

    local_in[3].wait()
    nbr_t[...] = nbr[...].T
    for t in range(3):
        for h in range(2):
            each(1, 4, lambda j, t=t, h=h: first(t, h, j, True).wait_recv())
            each(1, 4, lambda j, t=t, h=h: second(t, h, j, False).start())
    for h in range(2):
        each(1, 4, lambda j, h=h: second(0, h, j, True).wait_recv())
    third(0, False).start()
    third(0, True).wait_recv()

    def query_block(i):
        r = pl.ds(pl.multiple_of(i * 128, 128), 128)
        found = dot_nn(nbr[r, :], qw[...].reshape(1024, 512)).astype(BF)
        queries[pl.ds(2 * i, 2)] = found.reshape(2, 64, 512)

    each(0, 4, query_block)

    def slot_of(t):
        found = 0
        for s in range(8):
            found = found + jnp.where(shift[s % 2, s // 2] == t, s, 0)
        return jnp.minimum(found, 7)

    def query_send(t):
        qs[t] = queries[slot_of(t)]
        remote(qs.at[t], qr.at[t], qx_s.at[t], qx_r.at[t], at_n(16 - t)).start()

    each(1, 16, query_send)
    qr[0] = queries[slot_of(0)]

    local_in[6].wait()
    for h in range(8):
        turned = bias_raw[h]
        rolled = pltpu.roll(turned, 64, 1)
        lane = lax.broadcasted_iota(jnp.int32, (64, 128), 1)
        keep = (lane < 64) == (m == 0)
        bias_t[h * 64 : (h + 1) * 64, :] = jnp.where(keep, turned, rolled)

    for h in range(2):
        each(1, 4, lambda j, h=h: second(1, h, j, True).wait_recv())
    third(1, False).start()
    third(1, True).wait_recv()
    local_in[4].wait()

    def gmix_block(i):
        r = pl.ds(pl.multiple_of(i * 128, 128), 128)
        gmix[r, :] = dot_nt(cot[r, :], ow[...].reshape(512, 1024)).astype(BF)

    each(0, 4, gmix_block)

    for h in range(2):
        each(1, 4, lambda j, h=h: second(2, h, j, True).wait_recv())
    third(2, False).start()
    local_in[5].wait()
    third(2, True).wait_recv()

    gkv[...] = jnp.zeros_like(gkv)

    def kv_block(i):
        cols = pl.ds(pl.multiple_of(i * 512, 512), 512)
        gkv[...] += dot_nn(dec[:, cols], kvw[i // 4, i % 4].reshape(512, 1024))

    each(0, 8, kv_block)
    kv[...] = gkv[...].astype(BF)

    each(1, 16, lambda t: remote(qr.at[t], qr.at[t], qx_s.at[t], qx_r.at[t], at_n(t)).wait_recv())

    row_head = lax.broadcasted_iota(jnp.int32, (256, 256), 0) // 64
    col_head = lax.broadcasted_iota(jnp.int32, (256, 256), 1) // 64
    same = row_head == col_head

    def spread(block):
        return jnp.where(same, jnp.concatenate([block] * 4, axis=0), jnp.zeros((), BF))

    def gather_diag(full):
        kept = jnp.where(same, full, 0.0)
        return kept[0:64] + kept[64:128] + kept[128:192] + kept[192:256]

    def stretch(i):
        s = (i + 2 * (1 - m)) % 4
        q_both = jnp.concatenate([qr[shift[0, s]], qr[shift[1, s]]], axis=0)
        rows_kv = pl.ds(pl.multiple_of(s * 64, 64), 64)
        rows_tok = pl.ds(pl.multiple_of(s * 128, 128), 128)
        for g in range(2):
            lo, hi = g * 256, (g + 1) * 256
            keys = spread(kv[rows_kv, lo:hi])
            vals = spread(kv[rows_kv, 512 + lo : 512 + hi])
            q = q_both[:, lo:hi]
            gm = gmix[rows_tok, lo:hi]
            score = dot_nt(keys, q) * 0.125 + bias_t[lo:hi, :]
            grad_p = dot_nt(vals, gm)
            score = score.reshape(4, 64, 128)
            grad_p = grad_p.reshape(4, 64, 128)
            top = jnp.max(score, axis=1, keepdims=True)
            e = jnp.exp(score - top)
            w = e * (1.0 / jnp.sum(e, axis=1, keepdims=True))
            probs = w.astype(BF).reshape(256, 128)
            inner = jnp.sum(w * grad_p, axis=1, keepdims=True)
            gscore = (w * (grad_p - inner)).astype(BF).reshape(256, 128)
            mix[rows_tok, lo:hi] = dot_tn(probs, vals).astype(BF)
            gq = (dot_tn(gscore, keys) * 0.125).astype(BF)
            gq_loc[pl.ds(2 * s, 2), :, lo:hi] = gq.reshape(2, 64, 256)
            gkv[rows_kv, lo:hi] = gather_diag(dot_nn(gscore, q)) * 0.125
            gkv[rows_kv, 512 + lo : 512 + hi] = gather_diag(dot_nn(probs, gm))

    each(0, 2, stretch)
    gkv_s[...] = gkv[pl.ds(pl.multiple_of((1 - m) * 128, 128), 128), :].astype(BF)
    mp_copy = remote(gkv_s, gkv_r, mp_s.at[0], mp_r.at[0], at_mp)
    mp_copy.start()
    each(2, 4, stretch)

    def grad_send(t):
        gs[t] = gq_loc[slot_of(t)]
        remote(gs.at[t], gr.at[t], gx_s.at[t], gx_r.at[t], at_n(t)).start()

    each(1, 16, grad_send)
    gr[0] = gq_loc[slot_of(0)]

    mix_t = mix[...].T
    for p in range(2):
        block = dot_nn(mix_t[p * 256 : (p + 1) * 256], cot[...])
        ored[p] = block.astype(BF).reshape(4, 2, 2, 16, 1024)
    o1 = remote(ored.at[:, :, 1 - c], or1, r1_s.at[0], r1_r.at[0], at_core)
    o1.start()

    def att_block(i):
        r = pl.ds(pl.multiple_of(i * 128, 128), 128)
        att[r, :] = dot_nn(mix[r, :], ow[...].reshape(512, 1024)).astype(BF)

    each(0, 4, att_block)
    out_att = pltpu.make_async_copy(att, att_o, osem.at[0])
    out_att.start()

    o1.wait_recv()
    oa1[...] = (ored[:, :, c].astype(F32) + or1[...].astype(F32)).astype(BF)

    def o2(j):
        return remote(
            oa1.at[:, (y + j) % 4], or2.at[j], r2_s.at[0, j], r2_r.at[0, j], at_y(j)
        )

    each(1, 4, lambda j: o2(j).start())

    mp_copy.wait_recv()
    mine = pl.ds(pl.multiple_of(m * 128, 128), 128)
    kv_sum = (gkv[mine, :] + gkv_r[...].astype(F32)).astype(BF)
    gkv_s2 = kv_sum

    def rows_block(i):
        cols = pl.ds(pl.multiple_of(i * 512, 512), 512)
        rows[:, cols] = dot_nt(gkv_s2, kvw[i // 4, i % 4].reshape(512, 1024)).astype(BF)

    each(0, 8, rows_block)
    out_rows = pltpu.make_async_copy(rows, rows_o, osem.at[1])
    out_rows.start()

    each(1, 4, lambda j: o2(j).wait_recv())
    oa2[...] = (
        oa1[:, y].astype(F32) + or2[1].astype(F32) + or2[2].astype(F32) + or2[3].astype(F32)
    ).astype(BF)

    def o3(j):
        far = (x + j) % 4
        return remote(oa2.at[far // 2, far % 2], or3.at[j], r3_s.at[0, j], r3_r.at[0, j], at_x(j))

    each(1, 4, lambda j: o3(j).start())

    each(1, 16, lambda t: remote(gr.at[t], gr.at[t], gx_s.at[t], gx_r.at[t], at_n(t)).wait_recv())
    for s in range(8):
        gq_all[s * 64 : (s + 1) * 64, :] = gr[shift[s % 2, s // 2]]

    for p in range(2):
        block = dot_nn(nbr_t[p * 512 : (p + 1) * 512, :], gq_all[...])
        wred[p] = block.astype(BF).reshape(4, 2, 2, 32, 512)
    w1 = remote(wred.at[:, :, 1 - c], wr1, r1_s.at[1], r1_r.at[1], at_core)
    w1.start()

    def neigh_block(i):
        r = pl.ds(pl.multiple_of(i * 128, 128), 128)
        neigh[r, :] = dot_nt(gq_all[r, :], qw[...].reshape(1024, 512)).astype(BF)

    w1.wait_recv()
    wa1[...] = (wred[:, :, c].astype(F32) + wr1[...].astype(F32)).astype(BF)

    def w2(j):
        return remote(
            wa1.at[:, (y + j) % 4], wr2.at[j], r2_s.at[1, j], r2_r.at[1, j], at_y(j)
        )

    each(1, 4, lambda j: w2(j).start())
    each(0, 4, neigh_block)
    out_neigh = pltpu.make_async_copy(neigh, neigh_o, osem.at[2])
    out_neigh.start()
    each(1, 4, lambda j: w2(j).wait_recv())
    wa2[...] = (
        wa1[:, y].astype(F32) + wr2[1].astype(F32) + wr2[2].astype(F32) + wr2[3].astype(F32)
    ).astype(BF)

    def w3(j):
        far = (x + j) % 4
        return remote(wa2.at[far // 2, far % 2], wr3.at[j], r3_s.at[1, j], r3_r.at[1, j], at_x(j))

    each(1, 4, lambda j: w3(j).start())
    each(1, 4, lambda j: o3(j).wait_recv())
    o_sum = (
        oa2[xh, m].astype(F32) + or3[1].astype(F32) + or3[2].astype(F32) + or3[3].astype(F32)
    )
    each(1, 4, lambda j: w3(j).wait_recv())
    w_sum = (
        wa2[xh, m].astype(F32) + wr3[1].astype(F32) + wr3[2].astype(F32) + wr3[3].astype(F32)
    )
    for p in range(8):
        zs[p, 0:16] = w_sum[(p // 4) * 16 : (p // 4) * 16 + 16, (p % 4) * 128 : (p % 4) * 128 + 128].astype(BF)
        zs[p, 16:32] = o_sum[:, p * 128 : (p + 1) * 128].astype(BF)

    def z1(j):
        return remote(zs.at[(z + j) % 8], zr.at[j], r4_s.at[j], r4_r.at[j], at_z(j))

    each(1, 8, lambda j: z1(j).start())
    total = zs[z].astype(F32)
    each(1, 8, lambda j: z1(j).wait_recv())
    for j in range(1, 8):
        total = total + zr[j].astype(F32)
    za[...] = total.astype(BF)

    def z2(j, arriving):
        place = (z + 8 - j) % 8 if arriving else z
        return remote(za, zg.at[place], r5_s.at[j], r5_r.at[j], at_z(j))

    each(1, 8, lambda j: z2(j, False).start())
    zg[z] = za[...]
    each(1, 8, lambda j: z2(j, True).wait_recv())
    for p in range(8):
        gqw_v[(p // 4) * 16 : (p // 4) * 16 + 16, (p % 4) * 128 : (p % 4) * 128 + 128] = zg[p, 0:16].astype(F32)
        gow_v[:, p * 128 : (p + 1) * 128] = zg[p, 16:32].astype(F32)
    out_q = pltpu.make_async_copy(gqw_v, gqw_o, osem.at[3])
    out_o = pltpu.make_async_copy(gow_v, gow_o, osem.at[4])
    out_q.start()
    out_o.start()

    for t in range(3):
        for h in range(2):
            each(1, 4, lambda j, t=t, h=h: first(t, h, j, False).wait_send())
            each(1, 4, lambda j, t=t, h=h: second(t, h, j, False).wait_send())
        third(t, False).wait_send()
    each(1, 16, lambda t: remote(qs.at[t], qr.at[t], qx_s.at[t], qx_r.at[t], at_n(t)).wait_send())
    each(1, 16, lambda t: remote(gs.at[t], gr.at[t], gx_s.at[t], gx_r.at[t], at_n(t)).wait_send())
    mp_copy.wait_send()
    o1.wait_send()
    w1.wait_send()
    each(1, 4, lambda j: o2(j).wait_send())
    each(1, 4, lambda j: w2(j).wait_send())
    each(1, 4, lambda j: o3(j).wait_send())
    each(1, 4, lambda j: w3(j).wait_send())
    each(1, 8, lambda j: z1(j).wait_send())
    each(1, 8, lambda j: z2(j, False).wait_send())
    out_att.wait()
    out_rows.wait()
    out_neigh.wait()
    out_q.wait()
    out_o.wait()


def local(dec_rows, owner_shift, nbr_rows, cot_attended, query_w, kv_w, out_w, pos_bias):
    vmem = pltpu.VMEM
    dma = pltpu.SemaphoreType.DMA
    anywhere = pl.BlockSpec(memory_space=pl.ANY)
    scratch = [
        vmem((2, 4, 2, 2, 32, 512), BF), vmem((2, 4, 2, 2, 128, 1024), BF), vmem((2, 4, 2, 2, 16, 1024), BF),
        vmem((256, 4096), BF), vmem((512, 1024), BF), vmem((1024, 512), BF), vmem((512, 1024), BF),
        vmem((8, 64, 128), F32), vmem((512, 128), F32),
        vmem((8, 64, 512), BF), vmem((16, 64, 512), BF), vmem((16, 64, 512), BF), vmem((256, 1024), BF),
        vmem((512, 512), BF), vmem((512, 512), BF), vmem((8, 64, 512), BF),
        vmem((16, 64, 512), BF), vmem((16, 64, 512), BF), vmem((512, 512), BF),
        vmem((256, 1024), F32), vmem((128, 1024), BF), vmem((128, 1024), BF),
        vmem((512, 1024), BF), vmem((128, 4096), BF), vmem((512, 1024), BF),
        vmem((2, 4, 2, 2, 32, 512), BF), vmem((2, 4, 2, 2, 16, 1024), BF),
        vmem((2, 4, 2, 32, 512), BF), vmem((2, 4, 2, 16, 1024), BF),
        vmem((2, 4, 2, 32, 512), BF), vmem((2, 4, 2, 16, 1024), BF),
        vmem((4, 2, 2, 32, 512), BF), vmem((4, 2, 2, 16, 1024), BF),
        vmem((2, 2, 32, 512), BF), vmem((2, 2, 16, 1024), BF),
        vmem((4, 32, 512), BF), vmem((4, 16, 1024), BF),
        vmem((8, 32, 128), BF), vmem((8, 32, 128), BF), vmem((32, 128), BF), vmem((8, 32, 128), BF),
        vmem((32, 512), F32), vmem((16, 1024), F32),
        dma((7,)), dma((3, 3, 2, 4)), dma((3, 3, 2, 4)), dma((16,)), dma((16,)), dma((16,)), dma((16,)),
        dma((1,)), dma((1,)), dma((2,)), dma((2,)), dma((2, 4)), dma((2, 4)), dma((2, 4)), dma((2, 4)),
        dma((8,)), dma((8,)), dma((8,)), dma((8,)), dma((5,)),
    ]
    attended, grad_rows, grad_neigh, grad_query_w, grad_out_w = pl.pallas_call(
        kernel,
        out_shape=(
            jax.ShapeDtypeStruct((512, 1024), BF),
            jax.ShapeDtypeStruct((128, 4096), BF),
            jax.ShapeDtypeStruct((512, 1024), BF),
            jax.ShapeDtypeStruct((32, 512), F32),
            jax.ShapeDtypeStruct((16, 1024), F32),
        ),
        in_specs=[pl.BlockSpec(memory_space=pltpu.SMEM)] + [anywhere] * 7,
        out_specs=[anywhere] * 5,
        scratch_shapes=scratch,
        compiler_params=pltpu.CompilerParams(
            collective_id=0, has_side_effects=True, vmem_limit_bytes=60 * 2**20
        ),
        cost_estimate=pl.CostEstimate(flops=7 * 10**9, bytes_accessed=12 * 2**20, transcendentals=2 * 10**6),
        name="retrieval",
    )(
        owner_shift[0].T,
        dec_rows[0],
        nbr_rows.reshape(512, 1024),
        cot_attended.reshape(512, 1024),
        query_w,
        kv_w,
        out_w,
        jnp.swapaxes(pos_bias, 1, 2),
    )
    return (
        attended.reshape(1, 4, 2, 64, 1024),
        grad_rows[None],
        grad_neigh.reshape(1, 8, 64, 1024),
        grad_query_w,
        grad_out_w,
    )


def solution(mesh):
    placed = (
        P("dp", "nbr", None),
        P("dp", None, None),
        P("dp", "nbr", "mp", None),
        P("dp", "nbr", None, "mp", None),
        P(("nbr", "mp"), None),
        P(("nbr", "mp"), None),
        P(("nbr", "mp"), None),
        P(),
    )
    return jax.shard_map(
        local,
        mesh=mesh,
        in_specs=placed,
        out_specs=(
            P("dp", "nbr", None, "mp", None),
            P("dp", ("nbr", "mp"), None),
            P("dp", "nbr", "mp", None),
            P(("nbr", "mp"), None),
            P(("nbr", "mp"), None),
        ),
        check_vma=False,
    )
```

```python
import jax
import jax.numpy as jnp
from jax import lax
from jax.experimental import pallas as pl
from jax.experimental.pallas import tpu as pltpu
from jax.sharding import PartitionSpec as P

BF = jnp.bfloat16
F32 = jnp.float32
MESH = pl.DeviceIdType.MESH


def dot_nn(a, b):
    return lax.dot_general(a, b, (((1,), (0,)), ((), ())), preferred_element_type=F32)


def dot_nt(a, b):
    return lax.dot_general(a, b, (((1,), (1,)), ((), ())), preferred_element_type=F32)


def dot_tn(a, b):
    return lax.dot_general(a, b, (((0,), (0,)), ((), ())), preferred_element_type=F32)


def kernel(
    shift, dec_h, nbr_h, cot_h, wq_h, wkv_h, wo_h, bias_h,
    att_o, rows_o, neigh_o, gqw_o, gow_o,
    qw, kvw, ow, dec, nbr, nbr_t, cot, bias_raw, bias_t,
    queries, qs, qr, kv, gmix, mix, gq_loc, gs, gr_a, gr_b, gq_all,
    gkv, gkv_s, gkv_r, kv_sum, att, rows, neigh,
    wred, ored, wr1, or1, wa1, oa1, wr2y, wr2x, or2, wa2y, wa2x, oa2, wr3, or3, zs, zr, za, zg, gqw_v, gow_v,
    lsem, ag_s, ag_r, kv_ss, kv_rs, kc_s, kc_r, c_ss, c_rs, z_ss, z_rs, kz_s, kz_r, qx_s, qx_r, gx_s, gx_r, mp_s, mp_r,
    r1_s, r1_r, r2_s, r2_r, r3_s, r3_r, r4_s, r4_r, r5_s, r5_r, osem,
):
    z = lax.axis_index("dp")
    n = lax.axis_index("nbr")
    m = lax.axis_index("mp")
    xh = n // 8
    y = (n // 2) % 4
    c = n % 2
    x = xh * 2 + m

    def at_y(j):
        return {"nbr": xh * 8 + ((y + j) % 4) * 2 + c}

    def at_x(j):
        far = (x + j) % 4
        return {"nbr": (far // 2) * 8 + y * 2 + c, "mp": far % 2}

    def at_z(j):
        return {"dp": (z + j) % 8}

    def at_n(j):
        return {"nbr": (n + j) % 16}

    at_core = {"nbr": xh * 8 + y * 2 + (1 - c)}
    at_mp = {"mp": 1 - m}

    def remote(src, dst, ssem, rsem, device):
        return pltpu.make_async_remote_copy(
            src_ref=src, dst_ref=dst, send_sem=ssem, recv_sem=rsem, device_id=device, device_id_type=MESH
        )

    def each(lo, hi, body):
        lax.fori_loop(lo, hi, lambda j, carry: (body(j), carry)[1], 0)

    every = slice(None)

    def piece(place):
        return pl.ds(pl.multiple_of((place // 2) * 16, 16), 16), pl.ds(pl.multiple_of((place % 2) * 512, 512), 512)

    mine_z = piece(z)
    lower = pl.ds(64, 64)

    local_in = [
        pltpu.make_async_copy(wq_h, qw.at[xh, y, c, m], lsem.at[0]),
        pltpu.make_async_copy(wo_h, ow.at[xh, y, c, m], lsem.at[1]),
        pltpu.make_async_copy(wkv_h.at[mine_z], kvw.at[(xh, y, c, m) + mine_z], lsem.at[2]),
        pltpu.make_async_copy(nbr_h, nbr, lsem.at[3]),
        pltpu.make_async_copy(cot_h, cot, lsem.at[4]),
        pltpu.make_async_copy(dec_h, dec, lsem.at[5]),
        pltpu.make_async_copy(bias_h, bias_raw, lsem.at[6]),
        pltpu.make_async_copy(wkv_h.at[lower], kvw.at[xh, y, c, m, lower], lsem.at[7]),
    ]
    for one in local_in:
        one.start()

    barrier = pltpu.get_barrier_semaphore()
    each(1, 16, lambda j: pl.semaphore_signal(barrier, inc=1, device_id=at_n(j), device_id_type=MESH))
    each(1, 8, lambda j: pl.semaphore_signal(barrier, inc=1, device_id=at_z(j), device_id_type=MESH))
    pl.semaphore_signal(barrier, inc=1, device_id=at_x(1), device_id_type=MESH)
    pl.semaphore_signal(barrier, inc=1, device_id=at_x(3), device_id_type=MESH)
    pl.semaphore_wait(barrier, 24)

    halves = [
        (qw, [(pl.ds(0, 16), every), (pl.ds(16, 16), every)]),
        (ow, [(every, pl.ds(0, 512)), (every, pl.ds(512, 512))]),
    ]

    def first(t, h, j, arriving):
        buf, parts = halves[t]
        sy, sx, sm = y, xh, m
        if arriving:
            if h == 0:
                sy = (y + 4 - j) % 4
            else:
                far = (x + 4 - j) % 4
                sx, sm = far // 2, far % 2
        ref = buf.at[(sx, sy, c, sm) + parts[h]]
        return remote(ref, ref, ag_s.at[t, 0, h, j], ag_r.at[t, 0, h, j], at_y(j) if h == 0 else at_x(j))

    def second(t, h, j, arriving):
        buf, parts = halves[t]
        if h == 0:
            far = (x + 4 - j) % 4 if arriving else x
            ref = buf.at[(far // 2, every, c, far % 2) + parts[h]]
        else:
            sy = (y + 4 - j) % 4 if arriving else y
            ref = buf.at[(every, sy, c, every) + parts[h]]
        return remote(ref, ref, ag_s.at[t, 1, h, j], ag_r.at[t, 1, h, j], at_x(j) if h == 0 else at_y(j))

    def third(t, arriving):
        buf = halves[t][0]
        ref = buf.at[:, :, (1 - c) if arriving else c]
        return remote(ref, ref, ag_s.at[t, 2, 0, 0], ag_r.at[t, 2, 0, 0], at_core)

    def block(h, a1, a2, lo, count):
        px, py = (a2, a1) if h == 0 else (a1, a2)
        return kvw.at[px // 2, py, c, px % 2, pl.ds(64 + 32 * h + lo, count)]

    parts_of = ((0, 32), (0, 32), (0, 16), (16, 16))
    here = ((y, x), (x, y))
    at_axis = ((at_y, at_x), (at_x, at_y))

    def move(h, axis, b, kind, arriving):
        step = 1 if kind % 2 == 0 else 3
        off = 0 if kind < 2 else 4 - step
        if arriving:
            off = (off + 4 - step) % 4
        m1, m2 = here[h]
        if axis == 0:
            ref = block(h, (m1 + off) % 4, m2, *parts_of[kind])
        else:
            ref = block(h, (m1 + b) % 4, (m2 + off) % 4, *parts_of[kind])
        return remote(
            ref, ref, kv_ss.at[h, axis, b, kind], kv_rs.at[h, axis, b, kind], at_axis[h][axis](step)
        )

    def across(h, e, arriving):
        cc = (1 - c) if arriving else c
        a2 = (here[h][1] + e) % 4
        rows = pl.ds(64 + 32 * h, 32)
        if h == 0:
            ref = kvw.at[a2 // 2, :, cc, a2 % 2, rows]
        else:
            ref = kvw.at[:, a2, cc, :, rows]
        return remote(ref, ref, kc_s.at[h, e], kc_r.at[h, e], at_core)

    def plane_first(j, arriving):
        sy = (y + 4 - j) % 4 if arriving else y
        ref = kvw.at[(xh, sy, c, m) + mine_z]
        return remote(ref, ref, c_ss.at[0, j], c_rs.at[0, j], at_y(j))

    def plane_second(j, arriving):
        far = (x + 4 - j) % 4 if arriving else x
        ref = kvw.at[(far // 2, every, c, far % 2) + mine_z]
        return remote(ref, ref, c_ss.at[1, j], c_rs.at[1, j], at_x(j))

    def ring(k, way, sub, arriving):
        off = k if arriving else k - 1
        place = (z + (8 - off if way == 0 else off)) % 8
        ref = kvw.at[(sub, every, c, every) + piece(place)]
        return remote(ref, ref, z_ss.at[k, way, sub], z_rs.at[k, way, sub], at_z(1 if way == 0 else 7))

    def across_z(off, arriving):
        cc = (1 - c) if arriving else c
        ref = kvw.at[(every, every, cc, every) + piece((z + off) % 8)]
        return remote(ref, ref, kz_s.at[off], kz_r.at[off], at_core)

    def ring_pass(k, sub):
        for way in range(2):
            ring(k, way, sub, True).wait_recv()
            if k < 3 or (k == 3 and sub == way):
                ring(k + 1, way, sub, False).start()

    def move_pair(h, axis, b, first_kind, arriving):
        for kind in (first_kind, first_kind + 1):
            one = move(h, axis, b, kind, arriving)
            one.wait_recv() if arriving else one.start()

    local_in[2].wait()
    each(1, 4, lambda j: plane_first(j, False).start())
    local_in[0].wait()
    for h in range(2):
        each(1, 4, lambda j, h=h: first(0, h, j, False).start())
    local_in[7].wait()
    for h in range(2):
        move_pair(h, 0, 0, 0, False)
        move_pair(h, 1, 0, 0, False)
    local_in[1].wait()
    for h in range(2):
        each(1, 4, lambda j, h=h: first(1, h, j, False).start())

    each(1, 4, lambda j: plane_first(j, True).wait_recv())
    each(1, 4, lambda j: plane_second(j, False).start())
    for h in range(2):
        each(1, 4, lambda j, h=h: first(0, h, j, True).wait_recv())
        each(1, 4, lambda j, h=h: second(0, h, j, False).start())
    for h in range(2):
        each(1, 4, lambda j, h=h: first(1, h, j, True).wait_recv())
        each(1, 4, lambda j, h=h: second(1, h, j, False).start())
    for h in range(2):
        move_pair(h, 0, 0, 0, True)
        move_pair(h, 0, 0, 2, False)
        move_pair(h, 1, 3, 0, False)
        move_pair(h, 1, 1, 0, False)
    each(1, 4, lambda j: plane_second(j, True).wait_recv())
    for sub in range(2):
        for way in range(2):
            ring(1, way, sub, False).start()
    across_z(0, False).start()
    for h in range(2):
        each(1, 4, lambda j, h=h: second(0, h, j, True).wait_recv())
    third(0, False).start()
    for h in range(2):
        move_pair(h, 1, 0, 0, True)
        move_pair(h, 1, 0, 2, False)
    local_in[3].wait()
    third(0, True).wait_recv()

    def query_block(i):
        r = pl.ds(pl.multiple_of(i * 128, 128), 128)
        found = dot_nn(nbr[r, :], qw[...].reshape(1024, 512)).astype(BF)
        queries[pl.ds(2 * i, 2)] = found.reshape(2, 64, 512)

    each(0, 4, query_block)

    def slot_of(t):
        found = 0
        for s in range(8):
            found = found + jnp.where(shift[s % 2, s // 2] == t, s, 0)
        return jnp.minimum(found, 7)

    def query_send(t):
        qs[t] = queries[slot_of(t)]
        remote(qs.at[t], qr.at[t], qx_s.at[t], qx_r.at[t], at_n(16 - t)).start()

    each(1, 16, query_send)
    qr[0] = queries[slot_of(0)]

    ring_pass(1, 0)
    for h in range(2):
        move_pair(h, 0, 0, 2, True)
        move_pair(h, 1, 2, 0, False)
        across(h, 0, False).start()
    ring_pass(1, 1)
    across_z(1, False).start()
    across_z(7, False).start()

    local_in[6].wait()
    for h in range(8):
        turned = bias_raw[h]
        rolled = pltpu.roll(turned, 64, 1)
        lane = lax.broadcasted_iota(jnp.int32, (64, 128), 1)
        keep = (lane < 64) == (m == 0)
        bias_t[h * 64 : (h + 1) * 64, :] = jnp.where(keep, turned, rolled)

    for h in range(2):
        each(1, 4, lambda j, h=h: second(1, h, j, True).wait_recv())
    third(1, False).start()
    for b in (3, 1):
        for h in range(2):
            move_pair(h, 1, b, 0, True)
            move_pair(h, 1, b, 2, False)
    ring_pass(2, 0)
    third(1, True).wait_recv()
    local_in[4].wait()

    def gmix_block(i):
        r = pl.ds(pl.multiple_of(i * 128, 128), 128)
        gmix[r, :] = dot_nt(cot[r, :], ow[...].reshape(512, 1024)).astype(BF)

    each(0, 4, gmix_block)

    ring_pass(2, 1)
    across_z(2, False).start()
    across_z(6, False).start()
    for h in range(2):
        move_pair(h, 1, 2, 0, True)
        move_pair(h, 1, 2, 2, False)
        across(h, 3, False).start()
        across(h, 1, False).start()
    nbr_t[...] = nbr[...].T
    ring_pass(3, 0)
    ring_pass(3, 1)
    across_z(3, False).start()
    across_z(5, False).start()
    for h in range(2):
        for b in (0, 3, 1, 2):
            move_pair(h, 1, b, 2, True)
        across(h, 2, False).start()
    for way in range(2):
        ring(4, way, way, True).wait_recv()
    across_z(4, False).start()
    local_in[5].wait()
    each(0, 8, lambda off: across_z(off, True).wait_recv())
    for h in range(2):
        each(0, 4, lambda e, h=h: across(h, e, True).wait_recv())

    gkv[...] = jnp.zeros_like(gkv)

    def kv_block(i):
        cols = pl.ds(pl.multiple_of(i * 512, 512), 512)
        gkv[...] += dot_nn(dec[:, cols], kvw[i // 4, i % 4].reshape(512, 1024))

    each(0, 8, kv_block)
    kv[...] = gkv[...].astype(BF)

    each(1, 16, lambda t: remote(qr.at[t], qr.at[t], qx_s.at[t], qx_r.at[t], at_n(t)).wait_recv())

    row_head = lax.broadcasted_iota(jnp.int32, (256, 256), 0) // 64
    col_head = lax.broadcasted_iota(jnp.int32, (256, 256), 1) // 64
    same = row_head == col_head

    def spread(block):
        return jnp.where(same, jnp.concatenate([block] * 4, axis=0), jnp.zeros((), BF))

    def gather_diag(full):
        kept = jnp.where(same, full, 0.0)
        return kept[0:64] + kept[64:128] + kept[128:192] + kept[192:256]

    def stretch(s, lo, hi, g):
        q_both = jnp.concatenate([qr[shift[0, s]], qr[shift[1, s]]], axis=0)
        rows_kv = pl.ds(pl.multiple_of(s * 64, 64), 64)
        rows_tok = pl.ds(pl.multiple_of(s * 128, 128), 128)
        keys = spread(kv[rows_kv, lo:hi])
        vals = spread(kv[rows_kv, 512 + lo : 512 + hi])
        q = q_both[:, lo:hi]
        gm = gmix[rows_tok, lo:hi]
        score = dot_nt(keys, q) * 0.125 + bias_t[lo:hi, :]
        grad_p = dot_nt(vals, gm)
        score = score.reshape(4, 64, 128)
        grad_p = grad_p.reshape(4, 64, 128)
        top = jnp.max(score, axis=1, keepdims=True)
        e = jnp.exp(score - top)
        w = e * (1.0 / jnp.sum(e, axis=1, keepdims=True))
        probs = w.astype(BF).reshape(256, 128)
        inner = jnp.sum(w * grad_p, axis=1, keepdims=True)
        gscore = (w * (grad_p - inner)).astype(BF).reshape(256, 128)
        mix[rows_tok, lo:hi] = dot_tn(probs, vals).astype(BF)
        gq = (dot_tn(gscore, keys) * 0.125).astype(BF)
        gq_loc[g, pl.ds(2 * s, 2)] = gq.reshape(2, 64, 256)
        gkv[rows_kv, lo:hi] = gather_diag(dot_nn(gscore, q)) * 0.125
        gkv[rows_kv, 512 + lo : 512 + hi] = gather_diag(dot_nn(probs, gm))

    gr = (gr_a, gr_b)

    def grad_copy(g, t):
        return remote(gs.at[g, t], gr[g].at[t], gx_s.at[g, t], gx_r.at[g, t], at_n(t))

    def grad_send(g, t):
        gs[g, t] = gq_loc[g, slot_of(t)]
        grad_copy(g, t).start()

    other_rows = pl.ds(pl.multiple_of((1 - m) * 128, 128), 128)

    def mp_copy(g):
        return remote(gkv_s.at[g], gkv_r.at[g], mp_s.at[g], mp_r.at[g], at_mp)

    for g in range(2):
        lo, hi = g * 256, (g + 1) * 256
        each(0, 4, lambda s, g=g, lo=lo, hi=hi: stretch(s, lo, hi, g))
        if g == 1:
            mix_t = mix[...].T
            for p in range(2):
                part = dot_nn(mix_t[p * 256 : (p + 1) * 256], cot[...])
                ored[p] = part.astype(BF).reshape(4, 2, 2, 16, 1024)
            o1 = remote(ored.at[:, :, 1 - c], or1, r1_s.at[0], r1_r.at[0], at_core)
            o1.start()

        each(1, 16, lambda t, g=g: grad_send(g, t))
        gr[g][0] = gq_loc[g, slot_of(0)]
        gkv_s[g, :, 0:256] = gkv[other_rows, lo:hi].astype(BF)
        gkv_s[g, :, 256:512] = gkv[other_rows, 512 + lo : 512 + hi].astype(BF)
        mp_copy(g).start()

    def att_block(i):
        r = pl.ds(pl.multiple_of(i * 128, 128), 128)
        att[r, :] = dot_nn(mix[r, :], ow[...].reshape(512, 1024)).astype(BF)

    each(0, 4, att_block)
    out_att = pltpu.make_async_copy(att, att_o, osem.at[0])
    out_att.start()

    o1.wait_recv()
    oa1[...] = (ored[:, :, c].astype(F32) + or1[...].astype(F32)).astype(BF)

    def o2(j):
        return remote(
            oa1.at[:, (y + j) % 4], or2.at[j], r2_s.at[0, j], r2_r.at[0, j], at_y(j)
        )

    each(1, 4, lambda j: o2(j).start())

    def grads_back(g):
        lo, hi = g * 256, (g + 1) * 256
        each(1, 16, lambda t: grad_copy(g, t).wait_recv())
        for s in range(8):
            gq_all[s * 64 : (s + 1) * 64, lo:hi] = gr[g][shift[s % 2, s // 2]]
        for p in range(2):
            part = dot_nn(nbr_t[p * 512 : (p + 1) * 512, :], gq_all[:, lo:hi])
            wred[g, p] = part.astype(BF).reshape(4, 2, 2, 32, 256)
        w1(g).start()

    def w1(g):
        return remote(wred.at[g, :, :, 1 - c], wr1.at[g], r1_s.at[1 + g], r1_r.at[1 + g], at_core)

    def core_sum(g):
        w1(g).wait_recv()
        wa1[g] = (wred[g, :, :, c].astype(F32) + wr1[g].astype(F32)).astype(BF)

    def w2(g, j):
        far = (x + j) % 4
        if g == 0:
            src, dst, device = wa1.at[0, :, (y + j) % 4], wr2y.at[j], at_y(j)
        else:
            src, dst, device = wa1.at[1, far // 2, :, far % 2], wr2x.at[j], at_x(j)
        return remote(src, dst, r2_s.at[1 + g, j], r2_r.at[1 + g, j], device)

    def w3(g, j):
        far = (x + j) % 4
        if g == 0:
            src, device = wa2y.at[far // 2, far % 2], at_x(j)
        else:
            src, device = wa2x.at[(y + j) % 4], at_y(j)
        return remote(src, wr3.at[g, j], r3_s.at[1 + g, j], r3_r.at[1 + g, j], device)

    grads_back(0)

    def o3(j):
        far = (x + j) % 4
        return remote(oa2.at[far // 2, far % 2], or3.at[j], r3_s.at[0, j], r3_r.at[0, j], at_x(j))

    core_sum(0)
    each(1, 4, lambda j: w2(0, j).start())
    grads_back(1)
    core_sum(1)
    each(1, 4, lambda j: w2(1, j).start())
    each(1, 4, lambda j: o2(j).wait_recv())
    oa2[...] = (
        oa1[:, y].astype(F32) + or2[1].astype(F32) + or2[2].astype(F32) + or2[3].astype(F32)
    ).astype(BF)

    each(1, 4, lambda j: o3(j).start())
    each(1, 4, lambda j: w2(0, j).wait_recv())
    wa2y[...] = (
        wa1[0, :, y].astype(F32) + wr2y[1].astype(F32) + wr2y[2].astype(F32) + wr2y[3].astype(F32)
    ).astype(BF)
    each(1, 4, lambda j: w3(0, j).start())

    def neigh_block(i):
        r = pl.ds(pl.multiple_of(i * 128, 128), 128)
        neigh[r, :] = dot_nt(gq_all[r, :], qw[...].reshape(1024, 512)).astype(BF)

    each(0, 4, neigh_block)
    out_neigh = pltpu.make_async_copy(neigh, neigh_o, osem.at[2])
    out_neigh.start()

    each(1, 4, lambda j: w2(1, j).wait_recv())
    wa2x[...] = (
        wa1[1, xh, :, m].astype(F32) + wr2x[1].astype(F32) + wr2x[2].astype(F32) + wr2x[3].astype(F32)
    ).astype(BF)
    each(1, 4, lambda j: w3(1, j).start())

    mine = pl.ds(pl.multiple_of(m * 128, 128), 128)
    for g in range(2):
        lo, hi = g * 256, (g + 1) * 256
        mp_copy(g).wait_recv()
        kv_sum[:, lo:hi] = (gkv[mine, lo:hi] + gkv_r[g, :, 0:256].astype(F32)).astype(BF)
        kv_sum[:, 512 + lo : 512 + hi] = (
            gkv[mine, 512 + lo : 512 + hi] + gkv_r[g, :, 256:512].astype(F32)
        ).astype(BF)

    def rows_block(i):
        cols = pl.ds(pl.multiple_of(i * 512, 512), 512)
        rows[:, cols] = dot_nt(kv_sum[...], kvw[i // 4, i % 4].reshape(512, 1024)).astype(BF)

    each(1, 4, lambda j: o3(j).wait_recv())
    o_sum = (
        oa2[xh, m].astype(F32) + or3[1].astype(F32) + or3[2].astype(F32) + or3[3].astype(F32)
    )
    each(0, 4, rows_block)
    for g in range(2):
        each(1, 4, lambda j, g=g: w3(g, j).wait_recv())
        own = wa2y[xh, m] if g == 0 else wa2x[y]
        w_sum = own.astype(F32) + wr3[g, 1].astype(F32) + wr3[g, 2].astype(F32) + wr3[g, 3].astype(F32)
        for p in range(4):
            zs[4 * g + p, 0:16] = w_sum[(p // 2) * 16 : (p // 2) * 16 + 16, (p % 2) * 128 : (p % 2) * 128 + 128].astype(BF)
    for p in range(8):
        zs[p, 16:32] = o_sum[:, p * 128 : (p + 1) * 128].astype(BF)

    def z1(j):
        return remote(zs.at[(z + j) % 8], zr.at[j], r4_s.at[j], r4_r.at[j], at_z(j))

    each(1, 8, lambda j: z1(j).start())
    each(4, 8, rows_block)
    out_rows = pltpu.make_async_copy(rows, rows_o, osem.at[1])
    out_rows.start()
    total = zs[z].astype(F32)
    each(1, 8, lambda j: z1(j).wait_recv())
    for j in range(1, 8):
        total = total + zr[j].astype(F32)
    za[...] = total.astype(BF)

    def z2(j, arriving):
        place = (z + 8 - j) % 8 if arriving else z
        return remote(za, zg.at[place], r5_s.at[j], r5_r.at[j], at_z(j))

    each(1, 8, lambda j: z2(j, False).start())
    zg[z] = za[...]
    each(1, 8, lambda j: z2(j, True).wait_recv())
    for p in range(8):
        top_row, left = ((p // 2) % 2) * 16, (p // 4) * 256 + (p % 2) * 128
        gqw_v[top_row : top_row + 16, left : left + 128] = zg[p, 0:16].astype(F32)
        gow_v[:, p * 128 : (p + 1) * 128] = zg[p, 16:32].astype(F32)
    out_q = pltpu.make_async_copy(gqw_v, gqw_o, osem.at[3])
    out_o = pltpu.make_async_copy(gow_v, gow_o, osem.at[4])
    out_q.start()
    out_o.start()

    for t in range(2):
        for h in range(2):
            each(1, 4, lambda j, t=t, h=h: first(t, h, j, False).wait_send())
            each(1, 4, lambda j, t=t, h=h: second(t, h, j, False).wait_send())
        third(t, False).wait_send()
    each(1, 4, lambda j: plane_first(j, False).wait_send())
    each(1, 4, lambda j: plane_second(j, False).wait_send())
    for h in range(2):
        for kind in range(4):
            move(h, 0, 0, kind, False).wait_send()
            each(0, 4, lambda b, h=h, kind=kind: move(h, 1, b, kind, False).wait_send())
        each(0, 4, lambda e, h=h: across(h, e, False).wait_send())
    for k in range(1, 5):
        for way in range(2):
            for sub in range(2):
                if k < 4 or sub == way:
                    ring(k, way, sub, False).wait_send()
    each(0, 8, lambda off: across_z(off, False).wait_send())
    each(1, 16, lambda t: remote(qs.at[t], qr.at[t], qx_s.at[t], qx_r.at[t], at_n(t)).wait_send())
    for g in range(2):
        each(1, 16, lambda t, g=g: grad_copy(g, t).wait_send())
        mp_copy(g).wait_send()
        w1(g).wait_send()
    o1.wait_send()
    each(1, 4, lambda j: o2(j).wait_send())
    each(1, 4, lambda j: o3(j).wait_send())
    for g in range(2):
        each(1, 4, lambda j, g=g: w2(g, j).wait_send())
        each(1, 4, lambda j, g=g: w3(g, j).wait_send())
    each(1, 8, lambda j: z1(j).wait_send())
    each(1, 8, lambda j: z2(j, False).wait_send())
    out_att.wait()
    out_rows.wait()
    out_neigh.wait()
    out_q.wait()
    out_o.wait()


def hand_over(*refs):
    held, sem = refs[10:15], refs[15]
    into = [pltpu.make_async_copy(refs[i], held[i], sem.at[0, i]) for i in range(5)]
    out = [pltpu.make_async_copy(held[i], refs[5 + i], sem.at[1, i]) for i in range(5)]
    for one in into:
        one.start()
    for one, after in zip(into, out):
        one.wait()
        after.start()
    for one in out:
        one.wait()


def local(dec_rows, owner_shift, nbr_rows, cot_attended, query_w, kv_w, out_w, pos_bias):
    vmem = pltpu.VMEM
    dma = pltpu.SemaphoreType.DMA
    anywhere = pl.BlockSpec(memory_space=pl.ANY)
    scratch = [
        vmem((2, 4, 2, 2, 32, 512), BF), vmem((2, 4, 2, 2, 128, 1024), BF), vmem((2, 4, 2, 2, 16, 1024), BF),
        vmem((256, 4096), BF), vmem((512, 1024), BF), vmem((1024, 512), BF), vmem((512, 1024), BF),
        vmem((8, 64, 128), F32), vmem((512, 128), F32),
        vmem((8, 64, 512), BF), vmem((16, 64, 512), BF), vmem((16, 64, 512), BF), vmem((256, 1024), BF),
        vmem((512, 512), BF), vmem((512, 512), BF), vmem((2, 8, 64, 256), BF),
        vmem((2, 16, 64, 256), BF), vmem((16, 64, 256), BF), vmem((16, 64, 256), BF), vmem((512, 512), BF),
        vmem((256, 1024), F32), vmem((2, 128, 512), BF), vmem((2, 128, 512), BF), vmem((128, 1024), BF),
        vmem((512, 1024), BF), vmem((128, 4096), BF), vmem((512, 1024), BF),
        vmem((2, 2, 4, 2, 2, 32, 256), BF), vmem((2, 4, 2, 2, 16, 1024), BF),
        vmem((2, 2, 4, 2, 32, 256), BF), vmem((2, 4, 2, 16, 1024), BF),
        vmem((2, 2, 4, 2, 32, 256), BF), vmem((2, 4, 2, 16, 1024), BF),
        vmem((4, 2, 2, 32, 256), BF), vmem((4, 4, 32, 256), BF), vmem((4, 2, 2, 16, 1024), BF),
        vmem((2, 2, 32, 256), BF), vmem((4, 32, 256), BF), vmem((2, 2, 16, 1024), BF),
        vmem((2, 4, 32, 256), BF), vmem((4, 16, 1024), BF),
        vmem((8, 32, 128), BF), vmem((8, 32, 128), BF), vmem((32, 128), BF), vmem((8, 32, 128), BF),
        vmem((32, 512), F32), vmem((16, 1024), F32),
        dma((8,)), dma((2, 3, 2, 4)), dma((2, 3, 2, 4)), dma((2, 2, 4, 4)), dma((2, 2, 4, 4)), dma((2, 4)), dma((2, 4)),
        dma((2, 4)), dma((2, 4)), dma((5, 2, 2)), dma((5, 2, 2)), dma((8,)), dma((8,)),
        dma((16,)), dma((16,)), dma((2, 16)), dma((2, 16)),
        dma((2,)), dma((2,)), dma((3,)), dma((3,)), dma((3, 4)), dma((3, 4)), dma((3, 4)), dma((3, 4)),
        dma((8,)), dma((8,)), dma((8,)), dma((8,)), dma((5,)),
    ]
    shapes = (
        jax.ShapeDtypeStruct((512, 1024), BF),
        jax.ShapeDtypeStruct((128, 4096), BF),
        jax.ShapeDtypeStruct((512, 1024), BF),
        jax.ShapeDtypeStruct((32, 512), F32),
        jax.ShapeDtypeStruct((16, 1024), F32),
    )
    results = pl.pallas_call(
        kernel,
        out_shape=shapes,
        in_specs=[pl.BlockSpec(memory_space=pltpu.SMEM)] + [anywhere] * 7,
        out_specs=[anywhere] * 5,
        scratch_shapes=scratch,
        compiler_params=pltpu.CompilerParams(
            collective_id=0, has_side_effects=True, vmem_limit_bytes=60 * 2**20
        ),
        cost_estimate=pl.CostEstimate(flops=7 * 10**9, bytes_accessed=12 * 2**20, transcendentals=2 * 10**6),
        name="retrieval",
    )(
        owner_shift[0].T,
        dec_rows[0],
        nbr_rows.reshape(512, 1024),
        cot_attended.reshape(512, 1024),
        query_w,
        kv_w,
        out_w,
        jnp.swapaxes(pos_bias, 1, 2),
    )
    attended, grad_rows, grad_neigh, grad_query_w, grad_out_w = pl.pallas_call(
        hand_over,
        out_shape=shapes,
        in_specs=[anywhere] * 5,
        out_specs=[anywhere] * 5,
        scratch_shapes=[vmem(one.shape, one.dtype) for one in shapes] + [dma((2, 5))],
        name="hand_over",
    )(*results)
    return (
        attended.reshape(1, 4, 2, 64, 1024),
        grad_rows[None],
        grad_neigh.reshape(1, 8, 64, 1024),
        grad_query_w,
        grad_out_w,
    )


def solution(mesh):
    placed = (
        P("dp", "nbr", None),
        P("dp", None, None),
        P("dp", "nbr", "mp", None),
        P("dp", "nbr", None, "mp", None),
        P(("nbr", "mp"), None),
        P(("nbr", "mp"), None),
        P(("nbr", "mp"), None),
        P(),
    )
    return jax.shard_map(
        local,
        mesh=mesh,
        in_specs=placed,
        out_specs=(
            P("dp", "nbr", None, "mp", None),
            P("dp", ("nbr", "mp"), None),
            P("dp", "nbr", "mp", None),
            P(("nbr", "mp"), None),
            P(("nbr", "mp"), None),
        ),
        check_vma=False,
    )
```

```python
import jax
import jax.numpy as jnp
from jax import lax
from jax.experimental import pallas as pl
from jax.experimental.pallas import tpu as pltpu
from jax.sharding import PartitionSpec as P

BF = jnp.bfloat16
F32 = jnp.float32
MESH = pl.DeviceIdType.MESH


def dot_nn(a, b):
    return lax.dot_general(a, b, (((1,), (0,)), ((), ())), preferred_element_type=F32)


def dot_nt(a, b):
    return lax.dot_general(a, b, (((1,), (1,)), ((), ())), preferred_element_type=F32)


def dot_tn(a, b):
    return lax.dot_general(a, b, (((0,), (0,)), ((), ())), preferred_element_type=F32)


def kernel(
    shift, dec_h, nbr_h, cot_h, wq_h, wkv_h, wo_h, bias_h,
    att_o, rows_o, neigh_o, gqw_o, gow_o,
    qw, kvw, ow, dec, nbr, nbr_t, cot, bias_raw, bias_t,
    queries, qs, qr, kv, gmix, mix, gq_loc, gs, gr_a, gr_b, gq_all,
    kv_acc, gkv, gkv_s, gkv_r, kv_sum, att, rows, neigh,
    wred, ored, wr1, or1, wa1, oa1, wr2y, wr2x, or2, wa2y, wa2x, oa2, wr3, or3, zs, zr, za, zg, gqw_v, gow_v,
    lsem, ag_s, ag_r, kv_ss, kv_rs, kc_s, kc_r, c_ss, c_rs, z_ss, z_rs, kz_s, kz_r, qx_s, qx_r, gx_s, gx_r, mp_s, mp_r,
    r1_s, r1_r, r2_s, r2_r, r3_s, r3_r, r4_s, r4_r, r5_s, r5_r, osem,
):
    z = lax.axis_index("dp")
    n = lax.axis_index("nbr")
    m = lax.axis_index("mp")
    xh = n // 8
    y = (n // 2) % 4
    c = n % 2
    x = xh * 2 + m

    def at_y(j):
        return {"nbr": xh * 8 + ((y + j) % 4) * 2 + c}

    def at_x(j):
        far = (x + j) % 4
        return {"nbr": (far // 2) * 8 + y * 2 + c, "mp": far % 2}

    def at_z(j):
        return {"dp": (z + j) % 8}

    def at_n(j):
        return {"nbr": (n + j) % 16}

    at_core = {"nbr": xh * 8 + y * 2 + (1 - c)}
    at_mp = {"mp": 1 - m}

    def remote(src, dst, ssem, rsem, device):
        return pltpu.make_async_remote_copy(
            src_ref=src, dst_ref=dst, send_sem=ssem, recv_sem=rsem, device_id=device, device_id_type=MESH
        )

    def each(lo, hi, body):
        lax.fori_loop(lo, hi, lambda j, carry: (body(j), carry)[1], 0)

    every = slice(None)

    def piece(place):
        return pl.ds(pl.multiple_of((place // 2) * 16, 16), 16), pl.ds(pl.multiple_of((place % 2) * 512, 512), 512)

    mine_z = piece(z)
    lower = pl.ds(64, 64)

    local_in = [
        pltpu.make_async_copy(wq_h, qw.at[xh, y, c, m], lsem.at[0]),
        pltpu.make_async_copy(wo_h, ow.at[xh, y, c, m], lsem.at[1]),
        pltpu.make_async_copy(wkv_h.at[mine_z], kvw.at[(xh, y, c, m) + mine_z], lsem.at[2]),
        pltpu.make_async_copy(nbr_h, nbr, lsem.at[3]),
        pltpu.make_async_copy(cot_h, cot, lsem.at[4]),
        pltpu.make_async_copy(dec_h, dec, lsem.at[5]),
        pltpu.make_async_copy(bias_h, bias_raw, lsem.at[6]),
        pltpu.make_async_copy(wkv_h.at[lower], kvw.at[xh, y, c, m, lower], lsem.at[7]),
    ]
    for one in local_in:
        one.start()

    barrier = pltpu.get_barrier_semaphore()
    each(1, 16, lambda j: pl.semaphore_signal(barrier, inc=1, device_id=at_n(j), device_id_type=MESH))
    each(1, 8, lambda j: pl.semaphore_signal(barrier, inc=1, device_id=at_z(j), device_id_type=MESH))
    pl.semaphore_signal(barrier, inc=1, device_id=at_x(1), device_id_type=MESH)
    pl.semaphore_signal(barrier, inc=1, device_id=at_x(3), device_id_type=MESH)
    pl.semaphore_wait(barrier, 24)

    halves = [
        (qw, [(pl.ds(0, 16), every), (pl.ds(16, 16), every)]),
        (ow, [(every, pl.ds(0, 512)), (every, pl.ds(512, 512))]),
    ]

    def first(t, h, j, arriving):
        buf, parts = halves[t]
        sy, sx, sm = y, xh, m
        if arriving:
            if h == 0:
                sy = (y + 4 - j) % 4
            else:
                far = (x + 4 - j) % 4
                sx, sm = far // 2, far % 2
        ref = buf.at[(sx, sy, c, sm) + parts[h]]
        return remote(ref, ref, ag_s.at[t, 0, h, j], ag_r.at[t, 0, h, j], at_y(j) if h == 0 else at_x(j))

    def second(t, h, j, arriving):
        buf, parts = halves[t]
        if h == 0:
            far = (x + 4 - j) % 4 if arriving else x
            ref = buf.at[(far // 2, every, c, far % 2) + parts[h]]
        else:
            sy = (y + 4 - j) % 4 if arriving else y
            ref = buf.at[(every, sy, c, every) + parts[h]]
        return remote(ref, ref, ag_s.at[t, 1, h, j], ag_r.at[t, 1, h, j], at_x(j) if h == 0 else at_y(j))

    def third(t, arriving):
        buf = halves[t][0]
        ref = buf.at[:, :, (1 - c) if arriving else c]
        return remote(ref, ref, ag_s.at[t, 2, 0, 0], ag_r.at[t, 2, 0, 0], at_core)

    def block(h, a1, a2, lo, count):
        px, py = (a2, a1) if h == 0 else (a1, a2)
        return kvw.at[px // 2, py, c, px % 2, pl.ds(64 + 32 * h + lo, count)]

    parts_of = ((0, 32), (0, 32), (0, 16), (16, 16))
    here = ((y, x), (x, y))
    at_axis = ((at_y, at_x), (at_x, at_y))

    def move(h, axis, b, kind, arriving):
        step = 1 if kind % 2 == 0 else 3
        off = 0 if kind < 2 else 4 - step
        if arriving:
            off = (off + 4 - step) % 4
        m1, m2 = here[h]
        if axis == 0:
            ref = block(h, (m1 + off) % 4, m2, *parts_of[kind])
        else:
            ref = block(h, (m1 + b) % 4, (m2 + off) % 4, *parts_of[kind])
        return remote(
            ref, ref, kv_ss.at[h, axis, b, kind], kv_rs.at[h, axis, b, kind], at_axis[h][axis](step)
        )

    def across(h, e, arriving):
        cc = (1 - c) if arriving else c
        a2 = (here[h][1] + e) % 4
        rows = pl.ds(64 + 32 * h, 32)
        if h == 0:
            ref = kvw.at[a2 // 2, :, cc, a2 % 2, rows]
        else:
            ref = kvw.at[:, a2, cc, :, rows]
        return remote(ref, ref, kc_s.at[h, e], kc_r.at[h, e], at_core)

    def plane_first(j, arriving):
        sy = (y + 4 - j) % 4 if arriving else y
        ref = kvw.at[(xh, sy, c, m) + mine_z]
        return remote(ref, ref, c_ss.at[0, j], c_rs.at[0, j], at_y(j))

    def plane_second(j, arriving):
        far = (x + 4 - j) % 4 if arriving else x
        ref = kvw.at[(far // 2, every, c, far % 2) + mine_z]
        return remote(ref, ref, c_ss.at[1, j], c_rs.at[1, j], at_x(j))

    def ring(k, way, sub, arriving):
        off = k if arriving else k - 1
        place = (z + (8 - off if way == 0 else off)) % 8
        ref = kvw.at[(sub, every, c, every) + piece(place)]
        return remote(ref, ref, z_ss.at[k, way, sub], z_rs.at[k, way, sub], at_z(1 if way == 0 else 7))

    def across_z(off, arriving):
        cc = (1 - c) if arriving else c
        ref = kvw.at[(every, every, cc, every) + piece((z + off) % 8)]
        return remote(ref, ref, kz_s.at[off], kz_r.at[off], at_core)

    def ring_pass(k, sub):
        for way in range(2):
            ring(k, way, sub, True).wait_recv()
            if k < 3 or (k == 3 and sub == way):
                ring(k + 1, way, sub, False).start()

    def move_pair(h, axis, b, first_kind, arriving):
        for kind in (first_kind, first_kind + 1):
            one = move(h, axis, b, kind, arriving)
            one.wait_recv() if arriving else one.start()

    local_in[2].wait()
    each(1, 4, lambda j: plane_first(j, False).start())
    local_in[0].wait()
    for h in range(2):
        each(1, 4, lambda j, h=h: first(0, h, j, False).start())
    local_in[7].wait()
    for h in range(2):
        move_pair(h, 0, 0, 0, False)
        move_pair(h, 1, 0, 0, False)
    local_in[1].wait()
    for h in range(2):
        each(1, 4, lambda j, h=h: first(1, h, j, False).start())

    each(1, 4, lambda j: plane_first(j, True).wait_recv())
    each(1, 4, lambda j: plane_second(j, False).start())
    for h in range(2):
        each(1, 4, lambda j, h=h: first(0, h, j, True).wait_recv())
        each(1, 4, lambda j, h=h: second(0, h, j, False).start())
    for h in range(2):
        each(1, 4, lambda j, h=h: first(1, h, j, True).wait_recv())
        each(1, 4, lambda j, h=h: second(1, h, j, False).start())
    for h in range(2):
        move_pair(h, 0, 0, 0, True)
        move_pair(h, 0, 0, 2, False)
        move_pair(h, 1, 3, 0, False)
        move_pair(h, 1, 1, 0, False)
    each(1, 4, lambda j: plane_second(j, True).wait_recv())
    for sub in range(2):
        for way in range(2):
            ring(1, way, sub, False).start()
    across_z(0, False).start()
    for h in range(2):
        each(1, 4, lambda j, h=h: second(0, h, j, True).wait_recv())
    third(0, False).start()
    for h in range(2):
        move_pair(h, 1, 0, 0, True)
        move_pair(h, 1, 0, 2, False)
    local_in[3].wait()
    third(0, True).wait_recv()

    def query_block(i):
        r = pl.ds(pl.multiple_of(i * 128, 128), 128)
        found = dot_nn(nbr[r, :], qw[...].reshape(1024, 512)).astype(BF)
        queries[pl.ds(2 * i, 2)] = found.reshape(2, 64, 512)

    each(0, 4, query_block)

    def slot_of(t):
        found = 0
        for s in range(8):
            found = found + jnp.where(shift[s % 2, s // 2] == t, s, 0)
        return jnp.minimum(found, 7)

    def query_send(t):
        qs[t] = queries[slot_of(t)]
        remote(qs.at[t], qr.at[t], qx_s.at[t], qx_r.at[t], at_n(16 - t)).start()

    each(1, 16, query_send)
    qr[0] = queries[slot_of(0)]

    ring_pass(1, 0)
    for h in range(2):
        move_pair(h, 0, 0, 2, True)
        move_pair(h, 1, 2, 0, False)
        across(h, 0, False).start()
    ring_pass(1, 1)
    across_z(1, False).start()
    across_z(7, False).start()

    local_in[6].wait()
    for h in range(8):
        turned = bias_raw[h]
        rolled = pltpu.roll(turned, 64, 1)
        lane = lax.broadcasted_iota(jnp.int32, (64, 128), 1)
        keep = (lane < 64) == (m == 0)
        bias_t[h * 64 : (h + 1) * 64, :] = jnp.where(keep, turned, rolled)

    for h in range(2):
        each(1, 4, lambda j, h=h: second(1, h, j, True).wait_recv())
    third(1, False).start()
    for b in (3, 1):
        for h in range(2):
            move_pair(h, 1, b, 0, True)
            move_pair(h, 1, b, 2, False)
    ring_pass(2, 0)
    third(1, True).wait_recv()
    local_in[4].wait()

    def gmix_block(i):
        r = pl.ds(pl.multiple_of(i * 128, 128), 128)
        gmix[r, :] = dot_nt(cot[r, :], ow[...].reshape(512, 1024)).astype(BF)

    each(0, 4, gmix_block)

    ring_pass(2, 1)
    across_z(2, False).start()
    across_z(6, False).start()
    for h in range(2):
        move_pair(h, 1, 2, 0, True)
        move_pair(h, 1, 2, 2, False)
        across(h, 3, False).start()
        across(h, 1, False).start()
    nbr_t[...] = nbr[...].T
    ring_pass(3, 0)
    ring_pass(3, 1)
    across_z(3, False).start()
    across_z(5, False).start()
    for h in range(2):
        for b in (0, 3, 1, 2):
            move_pair(h, 1, b, 2, True)
        across(h, 2, False).start()
    for way in range(2):
        ring(4, way, way, True).wait_recv()
    across_z(4, False).start()
    local_in[5].wait()
    each(0, 8, lambda off: across_z(off, True).wait_recv())
    for h in range(2):
        each(0, 4, lambda e, h=h: across(h, e, True).wait_recv())

    def project(g):
        bands = [pl.ds(g * 256, 256), pl.ds(512 + g * 256, 256)]

        def kv_block(i):
            left = dec[:, pl.ds(pl.multiple_of(i * 1024, 1024), 1024)]
            for k, band in enumerate(bands):
                right = kvw[i // 2, pl.ds(2 * (i % 2), 2), :, :, :, band].reshape(1024, 256)
                kv_acc[:, k * 256 : (k + 1) * 256] += dot_nn(left, right)

        kv_acc[...] = jnp.zeros_like(kv_acc)
        each(0, 4, kv_block)
        for k, band in enumerate(bands):
            kv[:, band] = kv_acc[:, k * 256 : (k + 1) * 256].astype(BF)

    project(0)

    each(1, 16, lambda t: remote(qr.at[t], qr.at[t], qx_s.at[t], qx_r.at[t], at_n(t)).wait_recv())

    row_head = lax.broadcasted_iota(jnp.int32, (256, 256), 0) // 64
    col_head = lax.broadcasted_iota(jnp.int32, (256, 256), 1) // 64
    same = row_head == col_head

    def spread(block):
        return jnp.where(same, jnp.concatenate([block] * 4, axis=0), jnp.zeros((), BF))

    def gather_diag(full):
        kept = jnp.where(same, full, 0.0)
        return kept[0:64] + kept[64:128] + kept[128:192] + kept[192:256]

    def stretch(s, lo, hi, g):
        q_both = jnp.concatenate([qr[shift[0, s]], qr[shift[1, s]]], axis=0)
        rows_kv = pl.ds(pl.multiple_of(s * 64, 64), 64)
        rows_tok = pl.ds(pl.multiple_of(s * 128, 128), 128)
        keys = spread(kv[rows_kv, lo:hi])
        vals = spread(kv[rows_kv, 512 + lo : 512 + hi])
        q = q_both[:, lo:hi]
        gm = gmix[rows_tok, lo:hi]
        score = dot_nt(keys, q) * 0.125 + bias_t[lo:hi, :]
        grad_p = dot_nt(vals, gm)
        score = score.reshape(4, 64, 128)
        grad_p = grad_p.reshape(4, 64, 128)
        top = jnp.max(score, axis=1, keepdims=True)
        e = jnp.exp(score - top)
        w = e * (1.0 / jnp.sum(e, axis=1, keepdims=True))
        probs = w.astype(BF).reshape(256, 128)
        inner = jnp.sum(w * grad_p, axis=1, keepdims=True)
        gscore = (w * (grad_p - inner)).astype(BF).reshape(256, 128)
        mix[rows_tok, lo:hi] = dot_tn(probs, vals).astype(BF)
        gq = (dot_tn(gscore, keys) * 0.125).astype(BF)
        gq_loc[g, pl.ds(2 * s, 2)] = gq.reshape(2, 64, 256)
        gkv[rows_kv, lo:hi] = gather_diag(dot_nn(gscore, q)) * 0.125
        gkv[rows_kv, 512 + lo : 512 + hi] = gather_diag(dot_nn(probs, gm))

    gr = (gr_a, gr_b)

    def grad_copy(g, t):
        return remote(gs.at[g, t], gr[g].at[t], gx_s.at[g, t], gx_r.at[g, t], at_n(t))

    def grad_send(g, t):
        gs[g, t] = gq_loc[g, slot_of(t)]
        grad_copy(g, t).start()

    other_rows = pl.ds(pl.multiple_of((1 - m) * 128, 128), 128)

    def mp_copy(g):
        return remote(gkv_s.at[g], gkv_r.at[g], mp_s.at[g], mp_r.at[g], at_mp)

    for g in range(2):
        lo, hi = g * 256, (g + 1) * 256
        if g == 1:
            project(1)
        each(0, 4, lambda s, g=g, lo=lo, hi=hi: stretch(s, lo, hi, g))
        if g == 1:
            mix_t = mix[...].T
            for p in range(2):
                part = dot_nn(mix_t[p * 256 : (p + 1) * 256], cot[...])
                ored[p] = part.astype(BF).reshape(4, 2, 2, 16, 1024)
            o1 = remote(ored.at[:, :, 1 - c], or1, r1_s.at[0], r1_r.at[0], at_core)
            o1.start()

        each(1, 16, lambda t, g=g: grad_send(g, t))
        gr[g][0] = gq_loc[g, slot_of(0)]
        gkv_s[g, :, 0:256] = gkv[other_rows, lo:hi].astype(BF)
        gkv_s[g, :, 256:512] = gkv[other_rows, 512 + lo : 512 + hi].astype(BF)

    mp_copy(0).start()
    mp_copy(1).start()

    def att_block(i):
        r = pl.ds(pl.multiple_of(i * 128, 128), 128)
        att[r, :] = dot_nn(mix[r, :], ow[...].reshape(512, 1024)).astype(BF)

    each(0, 4, att_block)
    out_att = pltpu.make_async_copy(att, att_o, osem.at[0])
    out_att.start()

    o1.wait_recv()
    oa1[...] = (ored[:, :, c].astype(F32) + or1[...].astype(F32)).astype(BF)

    def o2(j):
        return remote(
            oa1.at[:, (y + j) % 4], or2.at[j], r2_s.at[0, j], r2_r.at[0, j], at_y(j)
        )

    each(1, 4, lambda j: o2(j).start())

    def grads_back(g):
        lo, hi = g * 256, (g + 1) * 256
        each(1, 16, lambda t: grad_copy(g, t).wait_recv())
        for s in range(8):
            gq_all[s * 64 : (s + 1) * 64, lo:hi] = gr[g][shift[s % 2, s // 2]]
        for p in range(2):
            part = dot_nn(nbr_t[p * 512 : (p + 1) * 512, :], gq_all[:, lo:hi])
            wred[g, p] = part.astype(BF).reshape(4, 2, 2, 32, 256)
        w1(g).start()

    def w1(g):
        return remote(wred.at[g, :, :, 1 - c], wr1.at[g], r1_s.at[1 + g], r1_r.at[1 + g], at_core)

    def core_sum(g):
        w1(g).wait_recv()
        wa1[g] = (wred[g, :, :, c].astype(F32) + wr1[g].astype(F32)).astype(BF)

    def w2(g, j):
        far = (x + j) % 4
        if g == 0:
            src, dst, device = wa1.at[0, :, (y + j) % 4], wr2y.at[j], at_y(j)
        else:
            src, dst, device = wa1.at[1, far // 2, :, far % 2], wr2x.at[j], at_x(j)
        return remote(src, dst, r2_s.at[1 + g, j], r2_r.at[1 + g, j], device)

    def w3(g, j):
        far = (x + j) % 4
        if g == 0:
            src, device = wa2y.at[far // 2, far % 2], at_x(j)
        else:
            src, device = wa2x.at[(y + j) % 4], at_y(j)
        return remote(src, wr3.at[g, j], r3_s.at[1 + g, j], r3_r.at[1 + g, j], device)

    grads_back(0)

    def o3(j):
        far = (x + j) % 4
        return remote(oa2.at[far // 2, far % 2], or3.at[j], r3_s.at[0, j], r3_r.at[0, j], at_x(j))

    core_sum(0)
    each(1, 4, lambda j: w2(0, j).start())
    grads_back(1)
    core_sum(1)
    each(1, 4, lambda j: w2(1, j).start())
    each(1, 4, lambda j: o2(j).wait_recv())
    oa2[...] = (
        oa1[:, y].astype(F32) + or2[1].astype(F32) + or2[2].astype(F32) + or2[3].astype(F32)
    ).astype(BF)

    each(1, 4, lambda j: o3(j).start())
    each(1, 4, lambda j: w2(0, j).wait_recv())
    wa2y[...] = (
        wa1[0, :, y].astype(F32) + wr2y[1].astype(F32) + wr2y[2].astype(F32) + wr2y[3].astype(F32)
    ).astype(BF)
    each(1, 4, lambda j: w3(0, j).start())

    def neigh_block(i):
        r = pl.ds(pl.multiple_of(i * 128, 128), 128)
        neigh[r, :] = dot_nt(gq_all[r, :], qw[...].reshape(1024, 512)).astype(BF)

    each(0, 4, neigh_block)
    out_neigh = pltpu.make_async_copy(neigh, neigh_o, osem.at[2])
    out_neigh.start()

    each(1, 4, lambda j: w2(1, j).wait_recv())
    wa2x[...] = (
        wa1[1, xh, :, m].astype(F32) + wr2x[1].astype(F32) + wr2x[2].astype(F32) + wr2x[3].astype(F32)
    ).astype(BF)
    each(1, 4, lambda j: w3(1, j).start())

    mine = pl.ds(pl.multiple_of(m * 128, 128), 128)
    for g in range(2):
        lo, hi = g * 256, (g + 1) * 256
        mp_copy(g).wait_recv()
        kv_sum[:, lo:hi] = (gkv[mine, lo:hi] + gkv_r[g, :, 0:256].astype(F32)).astype(BF)
        kv_sum[:, 512 + lo : 512 + hi] = (
            gkv[mine, 512 + lo : 512 + hi] + gkv_r[g, :, 256:512].astype(F32)
        ).astype(BF)

    def rows_block(i):
        cols = pl.ds(pl.multiple_of(i * 512, 512), 512)
        rows[:, cols] = dot_nt(kv_sum[...], kvw[i // 4, i % 4].reshape(512, 1024)).astype(BF)

    each(1, 4, lambda j: o3(j).wait_recv())
    o_sum = (
        oa2[xh, m].astype(F32) + or3[1].astype(F32) + or3[2].astype(F32) + or3[3].astype(F32)
    )
    each(0, 4, rows_block)
    for g in range(2):
        each(1, 4, lambda j, g=g: w3(g, j).wait_recv())
        own = wa2y[xh, m] if g == 0 else wa2x[y]
        w_sum = own.astype(F32) + wr3[g, 1].astype(F32) + wr3[g, 2].astype(F32) + wr3[g, 3].astype(F32)
        for p in range(4):
            zs[4 * g + p, 0:16] = w_sum[(p // 2) * 16 : (p // 2) * 16 + 16, (p % 2) * 128 : (p % 2) * 128 + 128].astype(BF)
    for p in range(8):
        zs[p, 16:32] = o_sum[:, p * 128 : (p + 1) * 128].astype(BF)

    def z1(j):
        return remote(zs.at[(z + j) % 8], zr.at[j], r4_s.at[j], r4_r.at[j], at_z(j))

    each(1, 8, lambda j: z1(j).start())
    each(4, 8, rows_block)
    out_rows = pltpu.make_async_copy(rows, rows_o, osem.at[1])
    out_rows.start()
    total = zs[z].astype(F32)
    each(1, 8, lambda j: z1(j).wait_recv())
    for j in range(1, 8):
        total = total + zr[j].astype(F32)
    za[...] = total.astype(BF)

    def z2(j, arriving):
        place = (z + 8 - j) % 8 if arriving else z
        return remote(za, zg.at[place], r5_s.at[j], r5_r.at[j], at_z(j))

    each(1, 8, lambda j: z2(j, False).start())
    zg[z] = za[...]
    each(1, 8, lambda j: z2(j, True).wait_recv())
    for p in range(8):
        top_row, left = ((p // 2) % 2) * 16, (p // 4) * 256 + (p % 2) * 128
        gqw_v[top_row : top_row + 16, left : left + 128] = zg[p, 0:16].astype(F32)
        gow_v[:, p * 128 : (p + 1) * 128] = zg[p, 16:32].astype(F32)
    out_q = pltpu.make_async_copy(gqw_v, gqw_o, osem.at[3])
    out_o = pltpu.make_async_copy(gow_v, gow_o, osem.at[4])
    out_q.start()
    out_o.start()

    for t in range(2):
        for h in range(2):
            each(1, 4, lambda j, t=t, h=h: first(t, h, j, False).wait_send())
            each(1, 4, lambda j, t=t, h=h: second(t, h, j, False).wait_send())
        third(t, False).wait_send()
    each(1, 4, lambda j: plane_first(j, False).wait_send())
    each(1, 4, lambda j: plane_second(j, False).wait_send())
    for h in range(2):
        for kind in range(4):
            move(h, 0, 0, kind, False).wait_send()
            each(0, 4, lambda b, h=h, kind=kind: move(h, 1, b, kind, False).wait_send())
        each(0, 4, lambda e, h=h: across(h, e, False).wait_send())
    for k in range(1, 5):
        for way in range(2):
            for sub in range(2):
                if k < 4 or sub == way:
                    ring(k, way, sub, False).wait_send()
    each(0, 8, lambda off: across_z(off, False).wait_send())
    each(1, 16, lambda t: remote(qs.at[t], qr.at[t], qx_s.at[t], qx_r.at[t], at_n(t)).wait_send())
    for g in range(2):
        each(1, 16, lambda t, g=g: grad_copy(g, t).wait_send())
        mp_copy(g).wait_send()
        w1(g).wait_send()
    o1.wait_send()
    each(1, 4, lambda j: o2(j).wait_send())
    each(1, 4, lambda j: o3(j).wait_send())
    for g in range(2):
        each(1, 4, lambda j, g=g: w2(g, j).wait_send())
        each(1, 4, lambda j, g=g: w3(g, j).wait_send())
    each(1, 8, lambda j: z1(j).wait_send())
    each(1, 8, lambda j: z2(j, False).wait_send())
    out_att.wait()
    out_rows.wait()
    out_neigh.wait()
    out_q.wait()
    out_o.wait()


def hand_over(*refs):
    held, sem = refs[10:15], refs[15]
    into = [pltpu.make_async_copy(refs[i], held[i], sem.at[0, i]) for i in range(5)]
    out = [pltpu.make_async_copy(held[i], refs[5 + i], sem.at[1, i]) for i in range(5)]
    for one in into:
        one.start()
    for one, after in zip(into, out):
        one.wait()
        after.start()
    for one in out:
        one.wait()


def local(dec_rows, owner_shift, nbr_rows, cot_attended, query_w, kv_w, out_w, pos_bias):
    vmem = pltpu.VMEM
    dma = pltpu.SemaphoreType.DMA
    anywhere = pl.BlockSpec(memory_space=pl.ANY)
    scratch = [
        vmem((2, 4, 2, 2, 32, 512), BF), vmem((2, 4, 2, 2, 128, 1024), BF), vmem((2, 4, 2, 2, 16, 1024), BF),
        vmem((256, 4096), BF), vmem((512, 1024), BF), vmem((1024, 512), BF), vmem((512, 1024), BF),
        vmem((8, 64, 128), F32), vmem((512, 128), F32),
        vmem((8, 64, 512), BF), vmem((16, 64, 512), BF), vmem((16, 64, 512), BF), vmem((256, 1024), BF),
        vmem((512, 512), BF), vmem((512, 512), BF), vmem((2, 8, 64, 256), BF),
        vmem((2, 16, 64, 256), BF), vmem((16, 64, 256), BF), vmem((16, 64, 256), BF), vmem((512, 512), BF),
        vmem((256, 512), F32), vmem((256, 1024), F32), vmem((2, 128, 512), BF), vmem((2, 128, 512), BF), vmem((128, 1024), BF),
        vmem((512, 1024), BF), vmem((128, 4096), BF), vmem((512, 1024), BF),
        vmem((2, 2, 4, 2, 2, 32, 256), BF), vmem((2, 4, 2, 2, 16, 1024), BF),
        vmem((2, 2, 4, 2, 32, 256), BF), vmem((2, 4, 2, 16, 1024), BF),
        vmem((2, 2, 4, 2, 32, 256), BF), vmem((2, 4, 2, 16, 1024), BF),
        vmem((4, 2, 2, 32, 256), BF), vmem((4, 4, 32, 256), BF), vmem((4, 2, 2, 16, 1024), BF),
        vmem((2, 2, 32, 256), BF), vmem((4, 32, 256), BF), vmem((2, 2, 16, 1024), BF),
        vmem((2, 4, 32, 256), BF), vmem((4, 16, 1024), BF),
        vmem((8, 32, 128), BF), vmem((8, 32, 128), BF), vmem((32, 128), BF), vmem((8, 32, 128), BF),
        vmem((32, 512), F32), vmem((16, 1024), F32),
        dma((8,)), dma((2, 3, 2, 4)), dma((2, 3, 2, 4)), dma((2, 2, 4, 4)), dma((2, 2, 4, 4)), dma((2, 4)), dma((2, 4)),
        dma((2, 4)), dma((2, 4)), dma((5, 2, 2)), dma((5, 2, 2)), dma((8,)), dma((8,)),
        dma((16,)), dma((16,)), dma((2, 16)), dma((2, 16)),
        dma((2,)), dma((2,)), dma((3,)), dma((3,)), dma((3, 4)), dma((3, 4)), dma((3, 4)), dma((3, 4)),
        dma((8,)), dma((8,)), dma((8,)), dma((8,)), dma((5,)),
    ]
    shapes = (
        jax.ShapeDtypeStruct((512, 1024), BF),
        jax.ShapeDtypeStruct((128, 4096), BF),
        jax.ShapeDtypeStruct((512, 1024), BF),
        jax.ShapeDtypeStruct((32, 512), F32),
        jax.ShapeDtypeStruct((16, 1024), F32),
    )
    results = pl.pallas_call(
        kernel,
        out_shape=shapes,
        in_specs=[pl.BlockSpec(memory_space=pltpu.SMEM)] + [anywhere] * 7,
        out_specs=[anywhere] * 5,
        scratch_shapes=scratch,
        compiler_params=pltpu.CompilerParams(
            collective_id=0, has_side_effects=True, vmem_limit_bytes=60 * 2**20
        ),
        cost_estimate=pl.CostEstimate(flops=7 * 10**9, bytes_accessed=12 * 2**20, transcendentals=2 * 10**6),
        name="retrieval",
    )(
        owner_shift[0].T,
        dec_rows[0],
        nbr_rows.reshape(512, 1024),
        cot_attended.reshape(512, 1024),
        query_w,
        kv_w,
        out_w,
        jnp.swapaxes(pos_bias, 1, 2),
    )
    attended, grad_rows, grad_neigh, grad_query_w, grad_out_w = pl.pallas_call(
        hand_over,
        out_shape=shapes,
        in_specs=[anywhere] * 5,
        out_specs=[anywhere] * 5,
        scratch_shapes=[vmem(one.shape, one.dtype) for one in shapes] + [dma((2, 5))],
        name="hand_over",
    )(*results)
    return (
        attended.reshape(1, 4, 2, 64, 1024),
        grad_rows[None],
        grad_neigh.reshape(1, 8, 64, 1024),
        grad_query_w,
        grad_out_w,
    )


def solution(mesh):
    placed = (
        P("dp", "nbr", None),
        P("dp", None, None),
        P("dp", "nbr", "mp", None),
        P("dp", "nbr", None, "mp", None),
        P(("nbr", "mp"), None),
        P(("nbr", "mp"), None),
        P(("nbr", "mp"), None),
        P(),
    )
    return jax.shard_map(
        local,
        mesh=mesh,
        in_specs=placed,
        out_specs=(
            P("dp", "nbr", None, "mp", None),
            P("dp", ("nbr", "mp"), None),
            P("dp", "nbr", "mp", None),
            P(("nbr", "mp"), None),
            P(("nbr", "mp"), None),
        ),
        check_vma=False,
    )
```

```python
import jax
import jax.numpy as jnp
from jax import lax
from jax.experimental import pallas as pl
from jax.experimental.pallas import tpu as pltpu
from jax.sharding import PartitionSpec as P

BF = jnp.bfloat16
F32 = jnp.float32
MESH = pl.DeviceIdType.MESH


def dot_nn(a, b):
    return lax.dot_general(a, b, (((1,), (0,)), ((), ())), preferred_element_type=F32)


def dot_nt(a, b):
    return lax.dot_general(a, b, (((1,), (1,)), ((), ())), preferred_element_type=F32)


def dot_tn(a, b):
    return lax.dot_general(a, b, (((0,), (0,)), ((), ())), preferred_element_type=F32)


def kernel(
    shift, dec_h, nbr_h, cot_h, wq_h, wkv_h, wo_h, bias_h,
    att_o, rows_o, neigh_o, gqw_o, gow_o,
    qw, kvw, ow, dec, nbr, nbr_t, cot, bias_raw, bias_t,
    queries, qs, qr, kv, gmix, mix, gq_loc, gs, gr_a, gr_b, gq_all,
    kv_acc, gkv, gkv_s, gkv_r, kv_sum, att, rows, neigh,
    wred, ored, wr1, or1, wa1, oa1, wr2y, wr2x, or2, wa2y, wa2x, oa2, wr3, or3, zs, zr, za, zg, gqw_v, gow_v,
    lsem, ag_s, ag_r, kv_ss, kv_rs, kc_s, kc_r, c_ss, c_rs, z_ss, z_rs, kz_s, kz_r, qx_s, qx_r, gx_s, gx_r, mp_s, mp_r,
    r1_s, r1_r, r2_s, r2_r, r3_s, r3_r, r4_s, r4_r, r5_s, r5_r, osem,
):
    z = lax.axis_index("dp")
    n = lax.axis_index("nbr")
    m = lax.axis_index("mp")
    xh = n // 8
    y = (n // 2) % 4
    c = n % 2
    x = xh * 2 + m

    def at_y(j):
        return {"nbr": xh * 8 + ((y + j) % 4) * 2 + c}

    def at_x(j):
        far = (x + j) % 4
        return {"nbr": (far // 2) * 8 + y * 2 + c, "mp": far % 2}

    def at_z(j):
        return {"dp": (z + j) % 8}

    def at_n(j):
        return {"nbr": (n + j) % 16}

    at_core = {"nbr": xh * 8 + y * 2 + (1 - c)}
    at_mp = {"mp": 1 - m}

    def remote(src, dst, ssem, rsem, device):
        return pltpu.make_async_remote_copy(
            src_ref=src, dst_ref=dst, send_sem=ssem, recv_sem=rsem, device_id=device, device_id_type=MESH
        )

    def each(lo, hi, body):
        lax.fori_loop(lo, hi, lambda j, carry: (body(j), carry)[1], 0)

    every = slice(None)

    def piece(place):
        return pl.ds(pl.multiple_of((place // 2) * 16, 16), 16), pl.ds(pl.multiple_of((place % 2) * 512, 512), 512)

    mine_z = piece(z)
    lower = pl.ds(64, 64)

    local_in = [
        pltpu.make_async_copy(wq_h, qw.at[xh, y, c, m], lsem.at[0]),
        pltpu.make_async_copy(wo_h, ow.at[xh, y, c, m], lsem.at[1]),
        pltpu.make_async_copy(wkv_h.at[mine_z], kvw.at[(xh, y, c, m) + mine_z], lsem.at[2]),
        pltpu.make_async_copy(nbr_h, nbr, lsem.at[3]),
        pltpu.make_async_copy(cot_h, cot, lsem.at[4]),
        pltpu.make_async_copy(dec_h, dec, lsem.at[5]),
        pltpu.make_async_copy(bias_h, bias_raw, lsem.at[6]),
        pltpu.make_async_copy(wkv_h.at[lower], kvw.at[xh, y, c, m, lower], lsem.at[7]),
    ]
    for one in local_in:
        one.start()

    barrier = pltpu.get_barrier_semaphore()
    each(1, 16, lambda j: pl.semaphore_signal(barrier, inc=1, device_id=at_n(j), device_id_type=MESH))
    each(1, 8, lambda j: pl.semaphore_signal(barrier, inc=1, device_id=at_z(j), device_id_type=MESH))
    pl.semaphore_signal(barrier, inc=1, device_id=at_x(1), device_id_type=MESH)
    pl.semaphore_signal(barrier, inc=1, device_id=at_x(3), device_id_type=MESH)
    pl.semaphore_wait(barrier, 24)

    halves = [
        (qw, [(pl.ds(0, 16), every), (pl.ds(16, 16), every)]),
        (ow, [(every, pl.ds(0, 512)), (every, pl.ds(512, 512))]),
    ]

    def first(t, h, j, arriving):
        buf, parts = halves[t]
        sy, sx, sm = y, xh, m
        if arriving:
            if h == 0:
                sy = (y + 4 - j) % 4
            else:
                far = (x + 4 - j) % 4
                sx, sm = far // 2, far % 2
        ref = buf.at[(sx, sy, c, sm) + parts[h]]
        return remote(ref, ref, ag_s.at[t, 0, h, j], ag_r.at[t, 0, h, j], at_y(j) if h == 0 else at_x(j))

    def second(t, h, j, arriving):
        buf, parts = halves[t]
        if h == 0:
            far = (x + 4 - j) % 4 if arriving else x
            ref = buf.at[(far // 2, every, c, far % 2) + parts[h]]
        else:
            sy = (y + 4 - j) % 4 if arriving else y
            ref = buf.at[(every, sy, c, every) + parts[h]]
        return remote(ref, ref, ag_s.at[t, 1, h, j], ag_r.at[t, 1, h, j], at_x(j) if h == 0 else at_y(j))

    def third(t, arriving):
        buf = halves[t][0]
        ref = buf.at[:, :, (1 - c) if arriving else c]
        return remote(ref, ref, ag_s.at[t, 2, 0, 0], ag_r.at[t, 2, 0, 0], at_core)

    def block(h, a1, a2, lo, count):
        px, py = (a2, a1) if h == 0 else (a1, a2)
        return kvw.at[px // 2, py, c, px % 2, pl.ds(64 + 32 * h + lo, count)]

    parts_of = ((0, 32), (0, 32), (0, 16), (16, 16))
    here = ((y, x), (x, y))
    at_axis = ((at_y, at_x), (at_x, at_y))

    def move(h, axis, b, kind, arriving):
        step = 1 if kind % 2 == 0 else 3
        off = 0 if kind < 2 else 4 - step
        if arriving:
            off = (off + 4 - step) % 4
        m1, m2 = here[h]
        if axis == 0:
            ref = block(h, (m1 + off) % 4, m2, *parts_of[kind])
        else:
            ref = block(h, (m1 + b) % 4, (m2 + off) % 4, *parts_of[kind])
        return remote(
            ref, ref, kv_ss.at[h, axis, b, kind], kv_rs.at[h, axis, b, kind], at_axis[h][axis](step)
        )

    def across(h, e, arriving):
        cc = (1 - c) if arriving else c
        a2 = (here[h][1] + e) % 4
        rows = pl.ds(64 + 32 * h, 32)
        if h == 0:
            ref = kvw.at[a2 // 2, :, cc, a2 % 2, rows]
        else:
            ref = kvw.at[:, a2, cc, :, rows]
        return remote(ref, ref, kc_s.at[h, e], kc_r.at[h, e], at_core)

    def plane_first(j, arriving):
        sy = (y + 4 - j) % 4 if arriving else y
        ref = kvw.at[(xh, sy, c, m) + mine_z]
        return remote(ref, ref, c_ss.at[0, j], c_rs.at[0, j], at_y(j))

    def plane_second(j, arriving):
        far = (x + 4 - j) % 4 if arriving else x
        ref = kvw.at[(far // 2, every, c, far % 2) + mine_z]
        return remote(ref, ref, c_ss.at[1, j], c_rs.at[1, j], at_x(j))

    def ring(k, way, sub, arriving):
        off = k if arriving else k - 1
        place = (z + (8 - off if way == 0 else off)) % 8
        ref = kvw.at[(sub, every, c, every) + piece(place)]
        return remote(ref, ref, z_ss.at[k, way, sub], z_rs.at[k, way, sub], at_z(1 if way == 0 else 7))

    def across_z(off, arriving):
        cc = (1 - c) if arriving else c
        ref = kvw.at[(every, every, cc, every) + piece((z + off) % 8)]
        return remote(ref, ref, kz_s.at[off], kz_r.at[off], at_core)

    def ring_pass(k, sub):
        for way in range(2):
            ring(k, way, sub, True).wait_recv()
            if k < 3 or (k == 3 and sub == way):
                ring(k + 1, way, sub, False).start()

    def move_pair(h, axis, b, first_kind, arriving):
        for kind in (first_kind, first_kind + 1):
            one = move(h, axis, b, kind, arriving)
            one.wait_recv() if arriving else one.start()

    local_in[2].wait()
    each(1, 4, lambda j: plane_first(j, False).start())
    local_in[0].wait()
    for h in range(2):
        each(1, 4, lambda j, h=h: first(0, h, j, False).start())
    local_in[7].wait()
    for h in range(2):
        move_pair(h, 0, 0, 0, False)
        move_pair(h, 1, 0, 0, False)
    local_in[1].wait()
    for h in range(2):
        each(1, 4, lambda j, h=h: first(1, h, j, False).start())

    each(1, 4, lambda j: plane_first(j, True).wait_recv())
    each(1, 4, lambda j: plane_second(j, False).start())
    for h in range(2):
        each(1, 4, lambda j, h=h: first(0, h, j, True).wait_recv())
        each(1, 4, lambda j, h=h: second(0, h, j, False).start())
    for h in range(2):
        each(1, 4, lambda j, h=h: first(1, h, j, True).wait_recv())
        each(1, 4, lambda j, h=h: second(1, h, j, False).start())
    for h in range(2):
        move_pair(h, 0, 0, 0, True)
        move_pair(h, 0, 0, 2, False)
        move_pair(h, 1, 3, 0, False)
        move_pair(h, 1, 1, 0, False)
    each(1, 4, lambda j: plane_second(j, True).wait_recv())
    for sub in range(2):
        for way in range(2):
            ring(1, way, sub, False).start()
    across_z(0, False).start()
    for h in range(2):
        each(1, 4, lambda j, h=h: second(0, h, j, True).wait_recv())
    third(0, False).start()
    for h in range(2):
        move_pair(h, 1, 0, 0, True)
        move_pair(h, 1, 0, 2, False)
    local_in[3].wait()
    third(0, True).wait_recv()

    def query_block(i):
        r = pl.ds(pl.multiple_of(i * 128, 128), 128)
        found = dot_nn(nbr[r, :], qw[...].reshape(1024, 512)).astype(BF)
        queries[pl.ds(2 * i, 2)] = found.reshape(2, 64, 512)

    each(0, 4, query_block)

    def slot_of(t):
        found = 0
        for s in range(8):
            found = found + jnp.where(shift[s % 2, s // 2] == t, s, 0)
        return jnp.minimum(found, 7)

    def query_send(t):
        qs[t] = queries[slot_of(t)]
        remote(qs.at[t], qr.at[t], qx_s.at[t], qx_r.at[t], at_n(16 - t)).start()

    each(1, 16, query_send)
    qr[0] = queries[slot_of(0)]

    ring_pass(1, 0)
    for h in range(2):
        move_pair(h, 0, 0, 2, True)
        move_pair(h, 1, 2, 0, False)
        across(h, 0, False).start()
    ring_pass(1, 1)
    across_z(1, False).start()
    across_z(7, False).start()

    local_in[6].wait()
    for h in range(8):
        turned = bias_raw[h]
        rolled = pltpu.roll(turned, 64, 1)
        lane = lax.broadcasted_iota(jnp.int32, (64, 128), 1)
        keep = (lane < 64) == (m == 0)
        bias_t[h * 64 : (h + 1) * 64, :] = jnp.where(keep, turned, rolled)

    for h in range(2):
        each(1, 4, lambda j, h=h: second(1, h, j, True).wait_recv())
    third(1, False).start()
    for b in (3, 1):
        for h in range(2):
            move_pair(h, 1, b, 0, True)
            move_pair(h, 1, b, 2, False)
    ring_pass(2, 0)
    third(1, True).wait_recv()
    local_in[4].wait()

    def gmix_block(i):
        r = pl.ds(pl.multiple_of(i * 128, 128), 128)
        gmix[r, :] = dot_nt(cot[r, :], ow[...].reshape(512, 1024)).astype(BF)

    each(0, 4, gmix_block)

    ring_pass(2, 1)
    across_z(2, False).start()
    across_z(6, False).start()
    for h in range(2):
        move_pair(h, 1, 2, 0, True)
        move_pair(h, 1, 2, 2, False)
        across(h, 3, False).start()
        across(h, 1, False).start()
    nbr_t[...] = nbr[...].T
    ring_pass(3, 0)
    ring_pass(3, 1)
    across_z(3, False).start()
    across_z(5, False).start()
    for h in range(2):
        for b in (0, 3, 1, 2):
            move_pair(h, 1, b, 2, True)
        across(h, 2, False).start()
    for way in range(2):
        ring(4, way, way, True).wait_recv()
    across_z(4, False).start()
    local_in[5].wait()
    each(0, 8, lambda off: across_z(off, True).wait_recv())
    for h in range(2):
        each(0, 4, lambda e, h=h: across(h, e, True).wait_recv())

    def project(g):
        bands = [pl.ds(g * 256, 256), pl.ds(512 + g * 256, 256)]

        def kv_block(i):
            left = dec[:, pl.ds(pl.multiple_of(i * 1024, 1024), 1024)]
            for k, band in enumerate(bands):
                right = kvw[i // 2, pl.ds(2 * (i % 2), 2), :, :, :, band].reshape(1024, 256)
                kv_acc[:, k * 256 : (k + 1) * 256] += dot_nn(left, right)

        kv_acc[...] = jnp.zeros_like(kv_acc)
        each(0, 4, kv_block)
        for k, band in enumerate(bands):
            kv[:, band] = kv_acc[:, k * 256 : (k + 1) * 256].astype(BF)

    project(0)

    each(1, 16, lambda t: remote(qr.at[t], qr.at[t], qx_s.at[t], qx_r.at[t], at_n(t)).wait_recv())

    row_head = lax.broadcasted_iota(jnp.int32, (256, 256), 0) // 64
    col_head = lax.broadcasted_iota(jnp.int32, (256, 256), 1) // 64
    same = row_head == col_head

    def spread(block):
        return jnp.where(same, jnp.concatenate([block] * 4, axis=0), jnp.zeros((), BF))

    def gather_diag(full):
        kept = jnp.where(same, full, 0.0)
        return kept[0:64] + kept[64:128] + kept[128:192] + kept[192:256]

    def stretch(s, lo, hi, g):
        q_both = jnp.concatenate([qr[shift[0, s]], qr[shift[1, s]]], axis=0)
        rows_kv = pl.ds(pl.multiple_of(s * 64, 64), 64)
        rows_tok = pl.ds(pl.multiple_of(s * 128, 128), 128)
        keys = spread(kv[rows_kv, lo:hi])
        vals = spread(kv[rows_kv, 512 + lo : 512 + hi])
        q = q_both[:, lo:hi]
        gm = gmix[rows_tok, lo:hi]
        score = dot_nt(keys, q) * 0.125 + bias_t[lo:hi, :]
        grad_p = dot_nt(vals, gm)
        score = score.reshape(4, 64, 128)
        grad_p = grad_p.reshape(4, 64, 128)
        top = jnp.max(score, axis=1, keepdims=True)
        e = jnp.exp(score - top)
        w = e * (1.0 / jnp.sum(e, axis=1, keepdims=True))
        probs = w.astype(BF).reshape(256, 128)
        inner = jnp.sum(w * grad_p, axis=1, keepdims=True)
        gscore = (w * (grad_p - inner)).astype(BF).reshape(256, 128)
        mix[rows_tok, lo:hi] = dot_tn(probs, vals).astype(BF)
        gq = (dot_tn(gscore, keys) * 0.125).astype(BF)
        gq_loc[g, pl.ds(2 * s, 2)] = gq.reshape(2, 64, 256)
        gkv[rows_kv, lo:hi] = gather_diag(dot_nn(gscore, q)) * 0.125
        gkv[rows_kv, 512 + lo : 512 + hi] = gather_diag(dot_nn(probs, gm))

    gr = (gr_a, gr_b)

    def grad_copy(g, t):
        return remote(gs.at[g, t], gr[g].at[t], gx_s.at[g, t], gx_r.at[g, t], at_n(t))

    def grad_send(g, t):
        gs[g, t] = gq_loc[g, slot_of(t)]
        grad_copy(g, t).start()

    other_rows = pl.ds(pl.multiple_of((1 - m) * 128, 128), 128)

    def mp_copy(g):
        return remote(gkv_s.at[g], gkv_r.at[g], mp_s.at[g], mp_r.at[g], at_mp)

    for g in range(2):
        lo, hi = g * 256, (g + 1) * 256
        if g == 1:
            project(1)
        each(0, 4, lambda s, g=g, lo=lo, hi=hi: stretch(s, lo, hi, g))
        if g == 1:
            mix_t = mix[...].T
            for p in range(2):
                part = dot_nn(mix_t[p * 256 : (p + 1) * 256], cot[...])
                ored[p] = part.astype(BF).reshape(4, 2, 2, 16, 1024)
            o1 = remote(ored.at[:, :, 1 - c], or1, r1_s.at[0], r1_r.at[0], at_core)
            o1.start()

        each(1, 16, lambda t, g=g: grad_send(g, t))
        gr[g][0] = gq_loc[g, slot_of(0)]
        gkv_s[g, :, 0:256] = gkv[other_rows, lo:hi].astype(BF)
        gkv_s[g, :, 256:512] = gkv[other_rows, 512 + lo : 512 + hi].astype(BF)

    mp_copy(0).start()
    mp_copy(1).start()

    def att_block(i):
        r = pl.ds(pl.multiple_of(i * 128, 128), 128)
        att[r, :] = dot_nn(mix[r, :], ow[...].reshape(512, 1024)).astype(BF)

    each(0, 4, att_block)
    out_att = pltpu.make_async_copy(att, att_o, osem.at[0])
    out_att.start()

    o1.wait_recv()
    oa1[...] = (ored[:, :, c].astype(F32) + or1[...].astype(F32)).astype(BF)

    def o2(j):
        return remote(
            oa1.at[:, (y + j) % 4], or2.at[j], r2_s.at[0, j], r2_r.at[0, j], at_y(j)
        )

    each(1, 4, lambda j: o2(j).start())

    def grads_back(g):
        lo, hi = g * 256, (g + 1) * 256
        each(1, 16, lambda t: grad_copy(g, t).wait_recv())
        for s in range(8):
            gq_all[s * 64 : (s + 1) * 64, lo:hi] = gr[g][shift[s % 2, s // 2]]
        for p in range(2):
            part = dot_nn(nbr_t[p * 512 : (p + 1) * 512, :], gq_all[:, lo:hi])
            wred[g, p] = part.astype(BF).reshape(4, 2, 2, 32, 256)
        w1(g).start()

    def w1(g):
        return remote(wred.at[g, :, :, 1 - c], wr1.at[g], r1_s.at[1 + g], r1_r.at[1 + g], at_core)

    def core_sum(g):
        w1(g).wait_recv()
        wa1[g] = (wred[g, :, :, c].astype(F32) + wr1[g].astype(F32)).astype(BF)

    def w2(g, j):
        far = (x + j) % 4
        if g == 0:
            src, dst, device = wa1.at[0, :, (y + j) % 4], wr2y.at[j], at_y(j)
        else:
            src, dst, device = wa1.at[1, far // 2, :, far % 2], wr2x.at[j], at_x(j)
        return remote(src, dst, r2_s.at[1 + g, j], r2_r.at[1 + g, j], device)

    def w3(g, j):
        far = (x + j) % 4
        if g == 0:
            src, device = wa2y.at[far // 2, far % 2], at_x(j)
        else:
            src, device = wa2x.at[(y + j) % 4], at_y(j)
        return remote(src, wr3.at[g, j], r3_s.at[1 + g, j], r3_r.at[1 + g, j], device)

    grads_back(0)

    def o3(j):
        far = (x + j) % 4
        return remote(oa2.at[far // 2, far % 2], or3.at[j], r3_s.at[0, j], r3_r.at[0, j], at_x(j))

    core_sum(0)
    each(1, 4, lambda j: w2(0, j).start())
    grads_back(1)
    core_sum(1)
    each(1, 4, lambda j: w2(1, j).start())
    each(1, 4, lambda j: o2(j).wait_recv())
    oa2[...] = (
        oa1[:, y].astype(F32) + or2[1].astype(F32) + or2[2].astype(F32) + or2[3].astype(F32)
    ).astype(BF)

    each(1, 4, lambda j: o3(j).start())
    each(1, 4, lambda j: w2(0, j).wait_recv())
    wa2y[...] = (
        wa1[0, :, y].astype(F32) + wr2y[1].astype(F32) + wr2y[2].astype(F32) + wr2y[3].astype(F32)
    ).astype(BF)
    each(1, 4, lambda j: w3(0, j).start())

    def neigh_block(i):
        r = pl.ds(pl.multiple_of(i * 128, 128), 128)
        neigh[r, :] = dot_nt(gq_all[r, :], qw[...].reshape(1024, 512)).astype(BF)

    each(0, 4, neigh_block)
    out_neigh = pltpu.make_async_copy(neigh, neigh_o, osem.at[2])
    out_neigh.start()

    each(1, 4, lambda j: w2(1, j).wait_recv())
    wa2x[...] = (
        wa1[1, xh, :, m].astype(F32) + wr2x[1].astype(F32) + wr2x[2].astype(F32) + wr2x[3].astype(F32)
    ).astype(BF)
    each(1, 4, lambda j: w3(1, j).start())

    mine = pl.ds(pl.multiple_of(m * 128, 128), 128)
    for g in range(2):
        lo, hi = g * 256, (g + 1) * 256
        mp_copy(g).wait_recv()
        kv_sum[:, lo:hi] = (gkv[mine, lo:hi] + gkv_r[g, :, 0:256].astype(F32)).astype(BF)
        kv_sum[:, 512 + lo : 512 + hi] = (
            gkv[mine, 512 + lo : 512 + hi] + gkv_r[g, :, 256:512].astype(F32)
        ).astype(BF)

    def rows_block(i):
        cols = pl.ds(pl.multiple_of(i * 512, 512), 512)
        rows[:, cols] = dot_nt(kv_sum[...], kvw[i // 4, i % 4].reshape(512, 1024)).astype(BF)

    each(1, 4, lambda j: o3(j).wait_recv())
    o_sum = (
        oa2[xh, m].astype(F32) + or3[1].astype(F32) + or3[2].astype(F32) + or3[3].astype(F32)
    )
    each(0, 4, rows_block)
    for g in range(2):
        each(1, 4, lambda j, g=g: w3(g, j).wait_recv())
        own = wa2y[xh, m] if g == 0 else wa2x[y]
        w_sum = own.astype(F32) + wr3[g, 1].astype(F32) + wr3[g, 2].astype(F32) + wr3[g, 3].astype(F32)
        for p in range(4):
            zs[4 * g + p, 0:16] = w_sum[(p // 2) * 16 : (p // 2) * 16 + 16, (p % 2) * 128 : (p % 2) * 128 + 128].astype(BF)
    for p in range(8):
        zs[p, 16:32] = o_sum[:, p * 128 : (p + 1) * 128].astype(BF)

    def z1(j):
        return remote(zs.at[(z + j) % 8], zr.at[j], r4_s.at[j], r4_r.at[j], at_z(j))

    each(1, 8, lambda j: z1(j).start())
    each(4, 8, rows_block)
    out_rows = pltpu.make_async_copy(rows, rows_o, osem.at[1])
    out_rows.start()
    for t in range(2):
        for h in range(2):
            each(1, 4, lambda j, t=t, h=h: first(t, h, j, False).wait_send())
            each(1, 4, lambda j, t=t, h=h: second(t, h, j, False).wait_send())
        third(t, False).wait_send()
    each(1, 4, lambda j: plane_first(j, False).wait_send())
    each(1, 4, lambda j: plane_second(j, False).wait_send())
    for h in range(2):
        for kind in range(4):
            move(h, 0, 0, kind, False).wait_send()
            each(0, 4, lambda b, h=h, kind=kind: move(h, 1, b, kind, False).wait_send())
        each(0, 4, lambda e, h=h: across(h, e, False).wait_send())
    for k in range(1, 5):
        for way in range(2):
            for sub in range(2):
                if k < 4 or sub == way:
                    ring(k, way, sub, False).wait_send()
    each(0, 8, lambda off: across_z(off, False).wait_send())
    total = zs[z].astype(F32)
    each(1, 8, lambda j: z1(j).wait_recv())
    for j in range(1, 8):
        total = total + zr[j].astype(F32)
    za[...] = total.astype(BF)

    def z2(j, arriving):
        place = (z + 8 - j) % 8 if arriving else z
        return remote(za, zg.at[place], r5_s.at[j], r5_r.at[j], at_z(j))

    each(1, 8, lambda j: z2(j, False).start())
    zg[z] = za[...]
    each(1, 16, lambda t: remote(qs.at[t], qr.at[t], qx_s.at[t], qx_r.at[t], at_n(t)).wait_send())
    for g in range(2):
        each(1, 16, lambda t, g=g: grad_copy(g, t).wait_send())
        mp_copy(g).wait_send()
        w1(g).wait_send()
    o1.wait_send()
    each(1, 4, lambda j: o2(j).wait_send())
    each(1, 4, lambda j: o3(j).wait_send())
    for g in range(2):
        each(1, 4, lambda j, g=g: w2(g, j).wait_send())
        each(1, 4, lambda j, g=g: w3(g, j).wait_send())
    each(1, 8, lambda j: z1(j).wait_send())
    out_att.wait()
    out_rows.wait()
    out_neigh.wait()
    each(1, 8, lambda j: z2(j, True).wait_recv())
    for p in range(8):
        top_row, left = ((p // 2) % 2) * 16, (p // 4) * 256 + (p % 2) * 128
        gqw_v[top_row : top_row + 16, left : left + 128] = zg[p, 0:16].astype(F32)
        gow_v[:, p * 128 : (p + 1) * 128] = zg[p, 16:32].astype(F32)
    out_q = pltpu.make_async_copy(gqw_v, gqw_o, osem.at[3])
    out_o = pltpu.make_async_copy(gow_v, gow_o, osem.at[4])
    out_q.start()
    out_o.start()

    each(1, 8, lambda j: z2(j, False).wait_send())
    out_q.wait()
    out_o.wait()


def hand_over(*refs):
    held, sem = refs[10:15], refs[15]
    into = [pltpu.make_async_copy(refs[i], held[i], sem.at[0, i]) for i in range(5)]
    out = [pltpu.make_async_copy(held[i], refs[5 + i], sem.at[1, i]) for i in range(5)]
    for one in into:
        one.start()
    for one, after in zip(into, out):
        one.wait()
        after.start()
    for one in out:
        one.wait()


def local(dec_rows, owner_shift, nbr_rows, cot_attended, query_w, kv_w, out_w, pos_bias):
    vmem = pltpu.VMEM
    dma = pltpu.SemaphoreType.DMA
    anywhere = pl.BlockSpec(memory_space=pl.ANY)
    scratch = [
        vmem((2, 4, 2, 2, 32, 512), BF), vmem((2, 4, 2, 2, 128, 1024), BF), vmem((2, 4, 2, 2, 16, 1024), BF),
        vmem((256, 4096), BF), vmem((512, 1024), BF), vmem((1024, 512), BF), vmem((512, 1024), BF),
        vmem((8, 64, 128), F32), vmem((512, 128), F32),
        vmem((8, 64, 512), BF), vmem((16, 64, 512), BF), vmem((16, 64, 512), BF), vmem((256, 1024), BF),
        vmem((512, 512), BF), vmem((512, 512), BF), vmem((2, 8, 64, 256), BF),
        vmem((2, 16, 64, 256), BF), vmem((16, 64, 256), BF), vmem((16, 64, 256), BF), vmem((512, 512), BF),
        vmem((256, 512), F32), vmem((256, 1024), F32), vmem((2, 128, 512), BF), vmem((2, 128, 512), BF), vmem((128, 1024), BF),
        vmem((512, 1024), BF), vmem((128, 4096), BF), vmem((512, 1024), BF),
        vmem((2, 2, 4, 2, 2, 32, 256), BF), vmem((2, 4, 2, 2, 16, 1024), BF),
        vmem((2, 2, 4, 2, 32, 256), BF), vmem((2, 4, 2, 16, 1024), BF),
        vmem((2, 2, 4, 2, 32, 256), BF), vmem((2, 4, 2, 16, 1024), BF),
        vmem((4, 2, 2, 32, 256), BF), vmem((4, 4, 32, 256), BF), vmem((4, 2, 2, 16, 1024), BF),
        vmem((2, 2, 32, 256), BF), vmem((4, 32, 256), BF), vmem((2, 2, 16, 1024), BF),
        vmem((2, 4, 32, 256), BF), vmem((4, 16, 1024), BF),
        vmem((8, 32, 128), BF), vmem((8, 32, 128), BF), vmem((32, 128), BF), vmem((8, 32, 128), BF),
        vmem((32, 512), F32), vmem((16, 1024), F32),
        dma((8,)), dma((2, 3, 2, 4)), dma((2, 3, 2, 4)), dma((2, 2, 4, 4)), dma((2, 2, 4, 4)), dma((2, 4)), dma((2, 4)),
        dma((2, 4)), dma((2, 4)), dma((5, 2, 2)), dma((5, 2, 2)), dma((8,)), dma((8,)),
        dma((16,)), dma((16,)), dma((2, 16)), dma((2, 16)),
        dma((2,)), dma((2,)), dma((3,)), dma((3,)), dma((3, 4)), dma((3, 4)), dma((3, 4)), dma((3, 4)),
        dma((8,)), dma((8,)), dma((8,)), dma((8,)), dma((5,)),
    ]
    shapes = (
        jax.ShapeDtypeStruct((512, 1024), BF),
        jax.ShapeDtypeStruct((128, 4096), BF),
        jax.ShapeDtypeStruct((512, 1024), BF),
        jax.ShapeDtypeStruct((32, 512), F32),
        jax.ShapeDtypeStruct((16, 1024), F32),
    )
    results = pl.pallas_call(
        kernel,
        out_shape=shapes,
        in_specs=[pl.BlockSpec(memory_space=pltpu.SMEM)] + [anywhere] * 7,
        out_specs=[anywhere] * 5,
        scratch_shapes=scratch,
        compiler_params=pltpu.CompilerParams(
            collective_id=0, has_side_effects=True, vmem_limit_bytes=60 * 2**20
        ),
        cost_estimate=pl.CostEstimate(flops=7 * 10**9, bytes_accessed=12 * 2**20, transcendentals=2 * 10**6),
        name="retrieval",
    )(
        owner_shift[0].T,
        dec_rows[0],
        nbr_rows.reshape(512, 1024),
        cot_attended.reshape(512, 1024),
        query_w,
        kv_w,
        out_w,
        jnp.swapaxes(pos_bias, 1, 2),
    )
    attended, grad_rows, grad_neigh, grad_query_w, grad_out_w = pl.pallas_call(
        hand_over,
        out_shape=shapes,
        in_specs=[anywhere] * 5,
        out_specs=[anywhere] * 5,
        scratch_shapes=[vmem(one.shape, one.dtype) for one in shapes] + [dma((2, 5))],
        name="hand_over",
    )(*results)
    return (
        attended.reshape(1, 4, 2, 64, 1024),
        grad_rows[None],
        grad_neigh.reshape(1, 8, 64, 1024),
        grad_query_w,
        grad_out_w,
    )


def solution(mesh):
    placed = (
        P("dp", "nbr", None),
        P("dp", None, None),
        P("dp", "nbr", "mp", None),
        P("dp", "nbr", None, "mp", None),
        P(("nbr", "mp"), None),
        P(("nbr", "mp"), None),
        P(("nbr", "mp"), None),
        P(),
    )
    return jax.shard_map(
        local,
        mesh=mesh,
        in_specs=placed,
        out_specs=(
            P("dp", "nbr", None, "mp", None),
            P("dp", ("nbr", "mp"), None),
            P("dp", "nbr", "mp", None),
            P(("nbr", "mp"), None),
            P(("nbr", "mp"), None),
        ),
        check_vma=False,
    )
```
